32 devices in a mesh: grp: 2 (over y), dom: 16 (over z, x, core).
Axes of the slice: x: 2, y: 2, z: 4, core: 2. Of those that a mesh axis runs over, the one named last changes fastest.
Arguments:
- atm_state: float32 [2, 16, 512, 2048], P(None, None, ('grp', 'dom')), may hold values from -6 to 6
- ocean_state: float32 [2, 16, 128, 512], P(None, None, 'dom', 'grp'), may hold values from -6 to 6
- atm_levels: float32 [16, 16], replicated, may hold values from -1.5 to 1.5
- ocean_levels: float32 [16, 16], replicated, may hold values from -1.5 to 1.5
- tile_weight: bfloat16 [8192, 128, 128], P(('grp', 'dom')), may hold values from 0 to 0.049804688
- tile_owner: int32 [8192, 1], P(('grp', 'dom')), may hold values from 0 to 31; in each aligned block of 256 rows (0 to 255, 256 to 511, ...) at most 12 rows name the same one
- tile_block: int32 [8192], P(('grp', 'dom')), may hold values from 0 to 15
- tile_source: int32 [8192], P(('grp', 'dom')), may hold values from 0 to 255
- tile_count: int32 [32], P(('grp', 'dom')), may hold values from 128 to 256, as said below
Outputs:
- atm_final: float32 [2, 16, 512, 2048], P(None, None, ('grp', 'dom'))
- ocean_final: float32 [2, 16, 128, 512], P(None, None, 'dom', 'grp')
The draws below stay inside these ranges and needn't reach their ends.
Inputs may be any that keep to these rules, and one draw needn't show every extreme that they name: `tile_owner`: among the 256 entries of one device's list, at most 12 name the same ocean device, live or not. `tile_count`: entries of a device's list at or past its count are padding and are ignored; some device's count is 256.
All inputs are finite; a program needn't handle non-finite values.
Results may differ from the reference program's by a relative error of at most 0.002.
Values may be sent and summed in bfloat16 or wider, within the bound.
A program may use at most 128 MiB of HBM per device.

```python
import math
import jax
import jax.numpy as jnp
import numpy as np
from jax import lax

LEV = 16
NVAR = 2
STEPS = 4
YA = 2048
XO_DEV = 8
YO_DEV = 256
TPD = 256
CAP = 12
ABPD = 256
OBPD = 16
XA = 512
XO = 128
YO = 512
N_GRP = 2
N_DOM = 16
DEVICES = 32


def draw_tile_count(key, part):
    key = jax.random.fold_in(key, 7)
    first, second = jax.random.split(key)
    counts = jax.random.randint(first, (DEVICES,), TPD // 2, TPD + 1)
    fullest = jax.random.randint(second, (), 0, DEVICES)
    return jnp.where(jnp.arange(DEVICES) == fullest, TPD, counts).astype(jnp.int32)


def plant(array, rng, smallest, top_value):
    dims = array.shape
    index_at = [jax.random.randint(jax.random.fold_in(rng, axis), (), 0, dims[axis]) for axis in range(len(dims))]
    array = array.at[tuple(index_at)].set(smallest)
    longest = dims.index(max(dims))
    index_at[longest] = (index_at[longest] + 1) % dims[longest]
    return array.at[tuple(index_at)].set(top_value)


def shard_levels(rng, dims, cuts, smallest, high):
    def one(dim, shards_of):
        draws = jax.random.uniform(jax.random.fold_in(jax.random.fold_in(rng, 6), dim), (shards_of,), jnp.float32, smallest / len(cuts), high / len(cuts))
        return jnp.repeat(jnp.exp(draws), dims[dim] // shards_of).reshape((-1,) + (1,) * (len(dims) - dim - 1))

    factor_of = one(*cuts[0])
    for cut in cuts[1:]:
        factor_of = factor_of * one(*cut)
    return factor_of


def deal_out(own_key, own, number, rows, number_of, top, most, slope):
    sequence = jax.random.permutation(own_key, number_of)
    packed, usual = load_shares(number_of, rows * top, most, slope, True), load_shares(number_of, rows * top, most, slope, False)
    places = jnp.arange(number_of)

    def named(sizes, offset_by):
        used = int((sizes > 0).sum())
        fixed = max(1, used // 4)
        moved = fixed + (places - fixed + offset_by * (used - fixed)) % max(1, number_of - fixed)
        return jnp.zeros((number_of,), jnp.int32).at[sequence[jnp.where(places < fixed, places, moved)]].set(jnp.asarray(sizes, jnp.int32))

    sizes = jnp.where(number % 4 == 0, named(packed, number // 4), named(usual, number - number // 4 - 1))
    mixed = jax.random.permutation(jax.random.fold_in(own, 3), number_of)
    source_of, sink = mixed[0:number_of // 2 * 2:2], mixed[1:number_of // 2 * 2:2]
    room = jnp.minimum(sizes[source_of] - 1, most - sizes[sink]) // 2
    room = jnp.where((source_of == sequence[0]) | (sink == sequence[0]) | (sizes[sink] == 0), 0, jnp.maximum(room, 0))
    moved = jax.random.randint(jax.random.fold_in(own, 4), (number_of // 2,), 0, 1 << 20) % (room + 1)
    sizes = sizes.at[source_of].add(-moved).at[sink].add(moved)
    items = jnp.searchsorted(jnp.cumsum(sizes), jnp.arange(rows * top), side="right").astype(jnp.int32)
    table = items.reshape(top, rows).T
    table = table[jax.random.permutation(jax.random.fold_in(own, 1), rows)]
    offset_by = jax.random.randint(jax.random.fold_in(own, 2), (rows, 1), 0, top)
    return jnp.take_along_axis(table, (jnp.arange(top)[None, :] + offset_by) % top, axis=1)


def load_shares(number_of, total, most, slope, full):
    portions = [(1 << 20) // math.isqrt(standing ** slope) + 1 for standing in range(1, number_of + 1)]
    largest = most if full else min(most, max(-(-total // number_of), total * portions[0] // sum(portions)))
    least = 1 if total - largest >= number_of - 1 else 0
    given, spare = [largest] + [least] * (number_of - 1), total - largest - least * (number_of - 1)
    while spare > 0:
        movable = [i for i in range(1, number_of) if given[i] < largest] or [i for i in range(1, number_of) if given[i] < most]
        pool, left = sum([portions[i] for i in movable]), spare
        for i in movable:
            addition = min(most - given[i], max(1, left * portions[i] // pool), spare)
            given[i] = given[i] + addition
            spare = spare - addition
    return np.array(given)


def scatter_about(rng, extent, width, reach, shards=(), held_as=jnp.bfloat16):
    drawn = jax.random.normal(rng, extent, jnp.float32) * width
    if len(shards) > 0:
        drawn = shard_levels(rng, extent, shards, -0.22, 0.18) * drawn
    return jnp.clip(drawn, min=-reach, max=reach).astype(held_as)


def setup_inputs(seed: int = 0) -> dict:
    key_of = jax.random.split(jax.random.key(seed), 10)
    atm_state = scatter_about(key_of[0], (NVAR, LEV, XA, YA), 1.0, 6.0, ((2, 32),), jnp.float32)
    ocean_state = scatter_about(key_of[1], (NVAR, LEV, XO, YO), 1.0, 6.0, ((2, 16), (3, 2)), jnp.float32)
    atm_levels = scatter_about(key_of[2], (LEV, LEV), LEV ** -0.5, 1.5, (), jnp.float32)
    ocean_levels = scatter_about(key_of[3], (LEV, LEV), LEV ** -0.5, 1.5, (), jnp.float32)
    tile_weight = jnp.clip(0.049804688 * jax.random.uniform(key_of[4], (DEVICES * TPD, 128, 128), jnp.float32) ** shard_levels(key_of[4], (DEVICES * TPD, 128, 128), ((0, 32),), -0.2, 0.2), 0.0, 0.049804688).astype(jnp.bfloat16)
    tile_owner_keys = jax.random.split(jax.random.fold_in(key_of[5], 1), (DEVICES * TPD) // TPD)
    tile_owner_turns = jax.random.permutation(jax.random.fold_in(key_of[5], 3), (DEVICES * TPD) // TPD)
    tile_owner = jax.vmap(lambda own, number: deal_out(jax.random.fold_in(key_of[5], 2), own, number, TPD, DEVICES, 1, CAP, 2))(tile_owner_keys, tile_owner_turns).reshape((DEVICES * TPD, 1))
    tile_block = plant(jax.random.randint(key_of[6], (DEVICES * TPD,), 0, OBPD), jax.random.fold_in(key_of[6], 1), 0, OBPD - 1).astype(jnp.int32)
    tile_source = plant(jax.random.randint(key_of[7], (DEVICES * TPD,), 0, ABPD), jax.random.fold_in(key_of[7], 1), 0, ABPD - 1).astype(jnp.int32)
    tile_count = draw_tile_count(jax.random.fold_in(key_of[9], 71), 0)
    return dict(atm_state=atm_state, ocean_state=ocean_state, atm_levels=atm_levels, ocean_levels=ocean_levels, tile_weight=tile_weight, tile_owner=tile_owner, tile_block=tile_block, tile_source=tile_source, tile_count=tile_count)


diffuse = 0.2
vertical = 0.25
couple = 0.5


def atmos_step(state, levels):
    along_x = jnp.roll(state, -1, axis=2) + jnp.roll(state, 1, axis=2)
    padded = jnp.pad(state, ((0, 0), (0, 0), (0, 0), (1, 1)))
    along_y = padded[..., 2:] + padded[..., :-2]
    mixing = jnp.einsum("lm,vmxy->vlxy", levels, state, precision=lax.Precision.HIGHEST)
    return state + diffuse * (along_x + along_y - 4.0 * state) + vertical * mixing


def ocean_step(state, levels):
    padded = jnp.pad(state, ((0, 0), (0, 0), (1, 1), (1, 1)))
    along_x = padded[:, :, 2:, 1:-1] + padded[:, :, :-2, 1:-1]
    along_y = padded[:, :, 1:-1, 2:] + padded[:, :, 1:-1, :-2]
    mixing = jnp.einsum("lm,vmxy->vlxy", levels, state, precision=lax.Precision.HIGHEST)
    return state + diffuse * (along_x + along_y - 4.0 * state) + vertical * mixing


def reference(atm_state, ocean_state, atm_levels, ocean_levels, tile_weight, tile_owner, tile_block, tile_source, tile_count):
    total = DEVICES * TPD
    surface = atm_state[:, 0].astype(jnp.bfloat16).reshape(NVAR, -1, 128).transpose(1, 0, 2)
    ocean_surface = ocean_state[:, 0].reshape(NVAR, N_DOM, XO_DEV, N_GRP, YO_DEV // 128, 128)
    ocean_blocks = ocean_surface.transpose(3, 1, 2, 4, 0, 5).reshape(DEVICES * OBPD, NVAR, 128)
    positions = jnp.arange(total, dtype=jnp.int32)
    alive = (positions % TPD) < jnp.repeat(tile_count, TPD)
    source = (positions // TPD) * ABPD + tile_source
    target = tile_owner[:, 0] * OBPD + tile_block
    weights = tile_weight.reshape(DEVICES, TPD, 128, 128)

    picked = surface[source].reshape(DEVICES, TPD, NVAR, 128)

    def forward(pair):
        return jnp.einsum("tfa,tao->tfo", pair[0].astype(jnp.float32), pair[1].astype(jnp.float32))

    forward_terms = lax.map(forward, (picked, weights)).reshape(total, NVAR, 128)
    forward_terms = jnp.where(alive[:, None, None], forward_terms, 0.0)
    received = jax.ops.segment_sum(forward_terms, target, num_segments=DEVICES * OBPD)
    flux = received - ocean_blocks
    flux_sent = flux.astype(jnp.bfloat16)

    flux_tiles = flux_sent[target].reshape(DEVICES, TPD, NVAR, 128)

    def backward(pair):
        return jnp.einsum("tfo,tao->tfa", pair[0].astype(jnp.float32), pair[1].astype(jnp.float32))

    back_terms = lax.map(backward, (flux_tiles, weights)).reshape(total, NVAR, 128)
    back_terms = jnp.where(alive[:, None, None], back_terms, 0.0)
    returned = jax.ops.segment_sum(back_terms, source, num_segments=DEVICES * ABPD)
    returned_field = returned.transpose(1, 0, 2).reshape(NVAR, XA, YA)

    flux_field = flux.reshape(N_GRP, N_DOM, XO_DEV, YO_DEV // 128, NVAR, 128)
    flux_field = flux_field.transpose(4, 1, 2, 0, 3, 5).reshape(NVAR, XO, YO)

    atmos = atm_state
    ocean = ocean_state
    for repeat in range(STEPS):
        atmos = atmos_step(atmos, atm_levels)
        ocean = ocean_step(ocean, ocean_levels)
    atm_final = atmos.at[:, 0].add(-couple * returned_field)
    ocean_final = ocean.at[:, 0].add(couple * flux_field)
    return atm_final, ocean_final
```

```python
import functools

import jax
import jax.numpy as jnp
from jax import lax
from jax.experimental import pallas as pl
from jax.experimental.pallas import tpu as pltpu
from jax.sharding import PartitionSpec as P

STEPS = 4
MESH = pl.DeviceIdType.MESH
F32, BF16, I32 = jnp.float32, jnp.bfloat16, jnp.int32

diffuse = 0.2
vertical = 0.25
couple = 0.5


def split(x):
    hi = x.astype(BF16)
    return hi, (x - hi.astype(F32)).astype(BF16)


def dot(a, b):
    return jnp.dot(a, b, preferred_element_type=F32)


def exact_dot(a, b):
    return jnp.dot(a, b, preferred_element_type=F32, precision=lax.Precision.HIGHEST)


def level_terms(levels):
    lev = levels.shape[0]
    size = lev * 8
    spread = (
        lax.broadcasted_iota(I32, (size, lev), 0) // 8 == lax.broadcasted_iota(I32, (size, lev), 1)
    ).astype(F32)
    spread_t = (
        lax.broadcasted_iota(I32, (lev, size), 1) // 8 == lax.broadcasted_iota(I32, (lev, size), 0)
    ).astype(F32)
    wide = exact_dot(exact_dot(spread, vertical * levels), spread_t)
    same = lax.broadcasted_iota(I32, (size, size), 0) % 8 == lax.broadcasted_iota(I32, (size, size), 1) % 8
    k1 = jnp.where(same, wide, 0.0)
    k2 = exact_dot(k1, k1)
    k3 = exact_dot(k2, k1)
    k4 = exact_dot(k2, k2)
    hi, lo = split(jnp.concatenate([4.0 * k1, 6.0 * k2, 4.0 * k3, k4], axis=0))
    return jnp.concatenate([hi, hi, lo], axis=1)


def mix(lhs, cells):
    lev, _, n = cells.shape
    hi, lo = split(cells.reshape(lev * 8, n))
    out = dot(lhs, jnp.concatenate([hi, lo, hi], axis=0))
    return out.reshape(lhs.shape[0] // (lev * 8), lev, 8, n)


def pack_pairs(cells):
    n2, _, n = cells.shape
    pairs = cells.reshape(n2 // 2, 2, 8, n)
    a, b = pairs[:, 0], pairs[:, 1]
    upper = lax.broadcasted_iota(I32, a.shape, 1) < 4
    top = jnp.where(upper, a, pltpu.roll(b, 4, 1))
    bottom = jnp.where(upper, pltpu.roll(a, 4, 1), b)
    return top, bottom


def halo_pair(high, low):
    upper = lax.broadcasted_iota(I32, high.shape, 0) < 4
    first = jnp.where(upper, high, pltpu.roll(low, 4, 0))
    second = jnp.where(upper, pltpu.roll(high, 4, 0), low)
    return first, second


def spread_groups(rows):
    which = lax.broadcasted_iota(I32, rows.shape, 0) % 8
    return jnp.concatenate([jnp.where(which == t, rows, 0.0).astype(BF16) for t in range(8)], axis=1)


def body(
    grid_shape,
    w_hbm, atm_hbm, ocean_ref, alev_ref, olev_ref, owner_ref, block_ref, source_ref, count_ref,
    out_hbm, oout_ref,
    w, atm, res, halo_src, halo_dst, halo, terms,
    o_src, o_dst, os_src, os_dst, om_src, om_dst, oext, oterms, o_lhs, a_lhs,
    tiles_f, contrib, acc, acc_in, send2, inbox, flux_all, ret,
    w_sem, atm_sem, out_sem, h_send, h_recv, o_send, o_recv, p1_sem, p2_send, p2_recv, p3_send, p3_recv, p4_sem,
):
    n_grp, n_dom = grid_shape
    nv, lev, rows, cols = atm.shape
    tiles = w.shape[0]
    chunks = cols // 128
    half = n_dom // 2
    nc = n_grp * half
    obl = send2.shape[0] // nc
    orow = ocean_ref.shape[2]
    ocol = ocean_ref.shape[3]
    g, j = lax.axis_index("grp"), lax.axis_index("dom")
    me = g * n_dom + j
    core = lax.rem(j, 2)
    chip = g * half + j // 2
    total = n_grp * n_dom

    def flat(d):
        return (d // n_dom, lax.rem(d, n_dom))

    def peer(k):
        c = lax.rem(chip + k, nc)
        return c, (c // half, lax.rem(c, half) * 2 + core)

    right, left = flat(lax.rem(me + 1, total)), flat(lax.rem(me + total - 1, total))
    partner = (g, j + 1 - 2 * core)
    up, down = (g, lax.rem(j + n_dom - 1, n_dom)), (g, lax.rem(j + 1, n_dom))
    side, side_up, side_down = (1 - g, j), (1 - g, up[1]), (1 - g, down[1])

    parts = w_sem.shape[0]
    per = tiles // parts

    def w_copy(c):
        span = pl.ds(c * per, per)
        return pltpu.make_async_copy(w_hbm.at[span], w.at[span], w_sem.at[c])

    def atm_copy(v):
        return pltpu.make_async_copy(atm_hbm.at[v], atm.at[v], atm_sem.at[v])

    for v in range(nv):
        atm_copy(v).start()
    for c in range(parts):
        w_copy(c).start()

    barrier = pltpu.get_barrier_semaphore()
    for who in (right, left, up, down, side, side_up, side_down):
        pl.semaphore_signal(barrier, inc=1, device_id=who, device_id_type=MESH)

    def greet(k, carry):
        pl.semaphore_signal(barrier, inc=1, device_id=peer(k)[1], device_id_type=MESH)
        return carry

    lax.fori_loop(1, nc, greet, 0)

    ocean = ocean_ref[...].reshape(nv * lev, orow, ocol)
    otop, obottom = pack_pairs(ocean)
    pairs = nv * lev // 2
    o_src[0] = otop.reshape(pairs * 8, ocol).astype(BF16)
    o_src[1] = obottom.reshape(pairs * 8, ocol).astype(BF16)

    def edge(x):
        return jnp.where(g == 0, x[..., ocol - 128:], x[..., :128])

    os_src[0] = edge(otop).reshape(pairs * 8, 128).astype(BF16)
    os_src[1] = edge(obottom).reshape(pairs * 8, 128).astype(BF16)
    om_src[...] = edge(ocean).reshape(nv * lev * 8, 128).astype(BF16)

    pl.semaphore_wait(barrier, 7 + nc - 1)

    def remote(src, dst, ssem, rsem, who):
        return pltpu.make_async_remote_copy(
            src_ref=src, dst_ref=dst, send_sem=ssem, recv_sem=rsem, device_id=who, device_id_type=MESH
        )

    o_copies = [
        remote(o_src.at[0], o_dst.at[0], o_send.at[0], o_recv.at[0], up),
        remote(o_src.at[1], o_dst.at[1], o_send.at[1], o_recv.at[1], down),
        remote(os_src.at[0], os_dst.at[0], o_send.at[2], o_recv.at[2], side_up),
        remote(os_src.at[1], os_dst.at[1], o_send.at[3], o_recv.at[3], side_down),
        remote(om_src, om_dst, o_send.at[4], o_recv.at[4], side),
    ]
    for copy in o_copies:
        copy.start()

    for v in range(nv):
        atm_copy(v).wait()
    h_copies = [
        remote(halo_src.at[0], halo_dst.at[0], h_send.at[0], h_recv.at[0], left),
        remote(halo_src.at[1], halo_dst.at[1], h_send.at[1], h_recv.at[1], right),
    ]

    def pack_halo(i, carry):
        v, pair = i // (lev // 4), lax.rem(i, lev // 4) * 4
        top, _ = pack_pairs(atm[v, pl.ds(pair, 4), 0:8, :])
        _, bottom = pack_pairs(atm[v, pl.ds(pair, 4), rows - 8:rows, :])
        span = pl.ds(pl.multiple_of(i * 16, 16), 16)
        halo_src[0, span, :] = top.reshape(16, cols).astype(BF16)
        halo_src[1, span, :] = bottom.reshape(16, cols).astype(BF16)
        return carry

    lax.fori_loop(0, nv * lev // 4, pack_halo, 0)
    for copy in h_copies:
        copy.start()

    nch = ocol // 128
    live = lax.broadcasted_iota(I32, (1, tiles), 1) < count_ref[0]
    owner, block, source = owner_ref[...], block_ref[...], source_ref[...]
    dest = (owner & 1) * (nc * obl) + (owner >> 1) * obl
    dest = dest + (block & (nch - 1)) * orow + (block >> (nch.bit_length() - 1))
    dest = jnp.where(live, dest, -1)
    place = (source & (chunks - 1)) * rows + (source >> (chunks.bit_length() - 1))
    place = jnp.where(live, place, -1)
    eye = lax.broadcasted_iota(I32, (tiles, tiles), 0) == lax.broadcasted_iota(I32, (tiles, tiles), 1)

    def column(x):
        return jnp.sum(jnp.where(eye, x.astype(F32), 0.0), axis=1, keepdims=True).astype(I32)

    dest_col, place_col = column(dest), column(place)
    nblk = chunks * rows
    pick = (lax.broadcasted_iota(I32, (tiles, nblk), 1) == place_col).astype(F32).astype(BF16)

    def as_blocks(v):
        field = atm[v, 0]
        return jnp.concatenate([field[:, c * 128:(c + 1) * 128] for c in range(chunks)], axis=0)

    surface = jnp.concatenate([as_blocks(v) for v in range(nv)], axis=1).astype(BF16)

    def tile_rows(values):
        values = values.reshape(tiles // 8, 8, nv * 128)
        tiles_f[...] = jnp.concatenate([values[:, :, v * 128:(v + 1) * 128] for v in range(nv)], axis=1)

    tile_rows(dot(pick, surface))
    pairs16 = tiles // 16

    def keep(i, out):
        for h in range(2):
            part = out[h * 16:(h + 1) * 16, h * 128:(h + 1) * 128]
            span = pl.ds(pl.multiple_of(i * 16 + h * 8, 8), 8)
            contrib[span, 0:128] = part[0:8]
            contrib[span, 128:256] = part[8:16]

    def forward(c, carry):
        w_copy(c).wait()
        for s in range(per // 16):
            i = c * (per // 16) + s
            lhs = jnp.concatenate([spread_groups(tiles_f[2 * i]), spread_groups(tiles_f[2 * i + 1])], axis=0)
            both = w[pl.ds(i * 16, 16)].reshape(2, 1024, 128)
            keep(i, dot(lhs, jnp.concatenate([both[0], both[1]], axis=1)))
        return carry

    lax.fori_loop(0, parts, forward, 0)

    chi, clo = split(contrib[...])
    span = nc * obl
    for h in range(2):
        hot = (lax.broadcasted_iota(I32, (span, tiles), 0) + h * span == dest).astype(F32).astype(BF16)
        acc[h] = dot(hot, chi) + dot(hot, clo)
    p1 = remote(acc.at[1 - core], acc_in, p1_sem.at[0], p1_sem.at[1], partner)
    p1.start()
    o_lhs[...] = level_terms(olev_ref[...])
    p1.wait_recv()
    own = acc[core] + acc_in[...]
    send2[...] = own.astype(BF16)

    def slot(ref, c):
        return ref.at[pl.ds(pl.multiple_of(c * obl, obl), obl)]

    def p2(k):
        c, who = peer(k)
        return remote(slot(send2, c), slot(inbox, chip), p2_send.at[c], p2_recv.at[chip], who)

    def p2_in(k):
        c, who = peer(k)
        return remote(slot(send2, c), slot(inbox, c), p2_send.at[c], p2_recv.at[c], who)

    def loop(f):
        def step(k, carry):
            f(k)
            return carry

        lax.fori_loop(1, nc, step, 0)

    loop(lambda k: p2(k).start())
    a_lhs[...] = level_terms(alev_ref[...])

    width = 512

    def atm_terms(v, t, rows_of, lhs):
        kinds = lhs.shape[0] // (lev * 8)

        def one(c, carry):
            at = pl.ds(pl.multiple_of(c * width, width), width)
            terms[0:kinds, :, t * 8:(t + 1) * 8, at] = mix(lhs, rows_of(at))
            return carry

        lax.fori_loop(0, cols // width, one, 0)

    for t in range(rows // 8):
        atm_terms(0, t, lambda at: atm[0, :, t * 8:(t + 1) * 8, at], a_lhs[...])

    mine = pl.ds(pl.multiple_of(chip * obl, obl), obl)
    loop(lambda k: p2_in(k).wait_recv())
    inbox[mine, :] = send2[mine, :]
    received = jnp.sum(inbox[...].astype(F32).reshape(nc, obl, nv * 128), axis=0)
    osurf = [
        jnp.concatenate([ocean_ref[v, 0, :, c * 128:(c + 1) * 128] for c in range(nch)], axis=0) for v in range(nv)
    ]
    flux = received - jnp.concatenate(osurf, axis=1)
    flux_all[core, mine, :] = flux.astype(BF16)

    def p3(k):
        c, who = peer(k)
        return remote(slot(flux_all.at[core], chip), slot(flux_all.at[core], chip), p3_send.at[c], p3_recv.at[chip], who)

    def p3_in(k):
        c, who = peer(k)
        return remote(slot(flux_all.at[core], c), slot(flux_all.at[core], c), p3_send.at[c], p3_recv.at[c], who)

    loop(lambda k: p3(k).start())

    for copy in o_copies:
        copy.wait_recv()
    for v in range(nv):
        m = nv * lev // 2 // nv
        top = jnp.concatenate([o_dst[0], os_dst[0]], axis=1).astype(F32).reshape(pairs, 8, ocol + 128)
        bottom = jnp.concatenate([o_dst[1], os_dst[1]], axis=1).astype(F32).reshape(pairs, 8, ocol + 128)
        beside = om_dst[...].astype(F32).reshape(nv, lev, 8, 128)
        oext[:, 0:8, 0:ocol] = ocean_ref[v]
        oext[:, 0:8, ocol:] = beside[v]
        for q in range(m):
            first, second = halo_pair(top[v * m + q], bottom[v * m + q])
            oext[2 * q, 8:16, :] = first
            oext[2 * q + 1, 8:16, :] = second
        for t in range(2):
            oterms[:, :, t * 8:(t + 1) * 8, :] = mix(o_lhs[...], oext[:, t * 8:(t + 1) * 8, :])
        shape = (16, ocol + 128)
        r_at, c_at = lax.broadcasted_iota(I32, shape, 0), lax.broadcasted_iota(I32, shape, 1)
        no_up = (r_at == 0) & (j == 0)
        no_down = (r_at == 7) & (j == n_dom - 1)
        no_left = (c_at == 0) & (g == 0)
        no_right = (c_at == ocol - 1) & (g == n_grp - 1)

        def ocean_level(l, carry):
            r = oext[l]
            for k in range(STEPS):
                total4 = jnp.where(no_up, 0.0, pltpu.roll(r, 1, 0)) + jnp.where(no_down, 0.0, pltpu.roll(r, 15, 0))
                total4 = total4 + jnp.where(no_left, 0.0, pltpu.roll(r, 1, 1))
                total4 = total4 + jnp.where(no_right, 0.0, pltpu.roll(r, ocol + 127, 1))
                r = diffuse * (r + total4) + oterms[k, l]
            oout_ref[v, l] = r[0:8, 0:ocol]
            return carry

        lax.fori_loop(0, lev, ocean_level, 0)
        field = jnp.concatenate([flux[c * 8:(c + 1) * 8, v * 128:(v + 1) * 128] for c in range(nch)], axis=1)
        oout_ref[v, 0] = oout_ref[v, 0] + couple * field

    loop(lambda k: p3_in(k).wait_recv())
    p4 = remote(flux_all.at[core], flux_all.at[core], p4_sem.at[0], p4_sem.at[1], partner)
    p4_in = remote(flux_all.at[1 - core], flux_all.at[1 - core], p4_sem.at[0], p4_sem.at[1], partner)
    p4.start()

    for copy in h_copies:
        copy.wait_recv()
    zeros = jnp.zeros((rows + 8, 128), F32)

    def out_copy(v):
        return pltpu.make_async_copy(res.at[v], out_hbm.at[v], out_sem.at[v])

    for v in range(nv):
        def unpack(i, carry):
            at = pl.ds(pl.multiple_of((v * lev // 4 + i) * 16, 16), 16)
            high, low = halo_dst[0, at, :].astype(F32), halo_dst[1, at, :].astype(F32)
            for q in range(2):
                first, second = halo_pair(high[q * 8:(q + 1) * 8], low[q * 8:(q + 1) * 8])
                halo[4 * i + 2 * q] = first
                halo[4 * i + 2 * q + 1] = second
            return carry

        lax.fori_loop(0, lev // 4, unpack, 0)
        if v > 0:
            for t in range(rows // 8):
                atm_terms(v, t, lambda at: atm[v, :, t * 8:(t + 1) * 8, at], a_lhs[...])
        atm_terms(v, rows // 8, lambda at: halo[:, :, at], a_lhs[0:3 * lev * 8, :])

        def atm_level(l, carry):
            r = jnp.concatenate([atm[v, l], halo[l]], axis=0)
            for k in range(STEPS):
                padded = jnp.concatenate([r, zeros], axis=1)
                along_y = pltpu.roll(padded, 1, 1)[:, :cols] + pltpu.roll(padded, cols + 127, 1)[:, :cols]
                along_x = pltpu.roll(r, 1, 0) + pltpu.roll(r, rows + 7, 0)
                r = r + along_x + along_y
                if k < STEPS - 1:
                    r = diffuse * r + terms[k, l]
                else:
                    r = diffuse * r[0:rows] + terms[k, l, 0:rows, :]
            res[v, l] = r
            return carry

        lax.fori_loop(0, lev, atm_level, 0)

    p4_in.wait_recv()
    hot = (lax.broadcasted_iota(I32, (tiles, 2 * span), 1) == dest_col).astype(F32).astype(BF16)
    tile_rows(dot(hot, flux_all[...].reshape(2 * span, nv * 128)))

    def backward(i, carry):
        lhs = jnp.concatenate([spread_groups(tiles_f[2 * i]), spread_groups(tiles_f[2 * i + 1])], axis=0)
        both = w[pl.ds(i * 16, 16)]
        rhs = jnp.concatenate(
            [jnp.concatenate([both[h * 8 + t] for t in range(8)], axis=1) for h in range(2)], axis=0
        )
        keep(i, lax.dot_general(lhs, rhs, (((1,), (1,)), ((), ())), preferred_element_type=F32))
        return carry

    lax.fori_loop(0, pairs16, backward, 0)
    bhi, blo = split(contrib[...])
    to_block = (lax.broadcasted_iota(I32, (nblk, tiles), 0) == place).astype(F32).astype(BF16)
    ret[...] = dot(to_block, bhi) + dot(to_block, blo)
    for v in range(nv):
        field = jnp.concatenate(
            [ret[c * rows:(c + 1) * rows, v * 128:(v + 1) * 128] for c in range(chunks)], axis=1
        )
        res[v, 0] = res[v, 0] - couple * field
        out_copy(v).start()

    for copy in o_copies + h_copies + [p1, p4]:
        copy.wait_send()
    loop(lambda k: p2(k).wait_send())
    loop(lambda k: p3(k).wait_send())
    for v in range(nv):
        out_copy(v).wait()


def solution(mesh):
    n_grp, n_dom = mesh.shape["grp"], mesh.shape["dom"]
    nc = n_grp * n_dom // 2

    def per_device(
        atm_state, ocean_state, atm_levels, ocean_levels, tile_weight, tile_owner, tile_block, tile_source, tile_count
    ):
        nv, lev, rows, cols = atm_state.shape
        tiles = tile_weight.shape[0]
        orow, ocol = ocean_state.shape[2:]
        obl = orow * ocol // 128
        pairs = nv * lev // 2
        lanes = nv * 128
        dma = pltpu.SemaphoreType.DMA
        vmem = pl.BlockSpec(memory_space=pltpu.VMEM)
        hbm = pl.BlockSpec(memory_space=pl.ANY)
        return pl.pallas_call(
            functools.partial(body, (n_grp, n_dom)),
            out_shape=(
                jax.ShapeDtypeStruct(atm_state.shape, F32),
                jax.ShapeDtypeStruct(ocean_state.shape, F32),
            ),
            in_specs=[hbm, hbm, vmem, vmem, vmem, vmem, vmem, vmem, pl.BlockSpec(memory_space=pltpu.SMEM)],
            out_specs=(hbm, vmem),
            scratch_shapes=[
                pltpu.VMEM(tile_weight.shape, BF16),
                pltpu.VMEM(atm_state.shape, F32),
                pltpu.VMEM(atm_state.shape, F32),
                pltpu.VMEM((2, pairs * 8, cols), BF16),
                pltpu.VMEM((2, pairs * 8, cols), BF16),
                pltpu.VMEM((lev, 8, cols), F32),
                pltpu.VMEM((STEPS, lev, rows + 8, cols), F32),
                pltpu.VMEM((2, pairs * 8, ocol), BF16),
                pltpu.VMEM((2, pairs * 8, ocol), BF16),
                pltpu.VMEM((2, pairs * 8, 128), BF16),
                pltpu.VMEM((2, pairs * 8, 128), BF16),
                pltpu.VMEM((nv * lev * 8, 128), BF16),
                pltpu.VMEM((nv * lev * 8, 128), BF16),
                pltpu.VMEM((lev, 16, ocol + 128), F32),
                pltpu.VMEM((STEPS, lev, 16, ocol + 128), F32),
                pltpu.VMEM((STEPS * lev * 8, 3 * lev * 8), BF16),
                pltpu.VMEM((STEPS * lev * 8, 3 * lev * 8), BF16),
                pltpu.VMEM((tiles // 8, 8 * nv, 128), F32),
                pltpu.VMEM((tiles, lanes), F32),
                pltpu.VMEM((2, nc * obl, lanes), F32),
                pltpu.VMEM((nc * obl, lanes), F32),
                pltpu.VMEM((nc * obl, lanes), BF16),
                pltpu.VMEM((nc * obl, lanes), BF16),
                pltpu.VMEM((2, nc * obl, lanes), BF16),
                pltpu.VMEM((rows * cols // 128, lanes), F32),
                dma((8,)), dma((nv,)), dma((nv,)),
                dma((2,)), dma((2,)), dma((5,)), dma((5,)),
                dma((2,)), dma((nc,)), dma((nc,)), dma((nc,)), dma((nc,)), dma((2,)),
            ],
            compiler_params=pltpu.CompilerParams(
                collective_id=0, has_side_effects=True, vmem_limit_bytes=60 * 1024 * 1024
            ),
            cost_estimate=pl.CostEstimate(flops=8_000_000_000, bytes_accessed=17_000_000, transcendentals=0),
        )(
            tile_weight, atm_state, ocean_state, atm_levels, ocean_levels,
            tile_owner.reshape(1, tiles), tile_block.reshape(1, tiles), tile_source.reshape(1, tiles), tile_count,
        )

    in_specs = (
        P(None, None, ("grp", "dom"), None),
        P(None, None, "dom", "grp"),
        P(),
        P(),
        P(("grp", "dom"), None, None),
        P(("grp", "dom"), None),
        P(("grp", "dom")),
        P(("grp", "dom")),
        P(("grp", "dom")),
    )
    out_specs = (P(None, None, ("grp", "dom"), None), P(None, None, "dom", "grp"))
    return jax.shard_map(per_device, mesh=mesh, in_specs=in_specs, out_specs=out_specs, check_vma=False)
```

```python
import functools

import jax
import jax.numpy as jnp
from jax import lax
from jax.experimental import pallas as pl
from jax.experimental.pallas import tpu as pltpu
from jax.sharding import PartitionSpec as P

STEPS = 4
MESH = pl.DeviceIdType.MESH
F32, BF16, I32 = jnp.float32, jnp.bfloat16, jnp.int32

diffuse = 0.2
vertical = 0.25
couple = 0.5


def split(x):
    hi = x.astype(BF16)
    return hi, (x - hi.astype(F32)).astype(BF16)


def dot(a, b):
    return jnp.dot(a, b, preferred_element_type=F32)


def exact_dot(a, b):
    return jnp.dot(a, b, preferred_element_type=F32, precision=lax.Precision.HIGHEST)


def level_terms(levels):
    lev = levels.shape[0]
    size = lev * 8
    spread = (
        lax.broadcasted_iota(I32, (size, lev), 0) // 8 == lax.broadcasted_iota(I32, (size, lev), 1)
    ).astype(F32)
    spread_t = (
        lax.broadcasted_iota(I32, (lev, size), 1) // 8 == lax.broadcasted_iota(I32, (lev, size), 0)
    ).astype(F32)
    wide = exact_dot(exact_dot(spread, vertical * levels), spread_t)
    same = lax.broadcasted_iota(I32, (size, size), 0) % 8 == lax.broadcasted_iota(I32, (size, size), 1) % 8
    k1 = jnp.where(same, wide, 0.0)
    k2 = exact_dot(k1, k1)
    k3 = exact_dot(k2, k1)
    k4 = exact_dot(k2, k2)
    hi, lo = split(jnp.concatenate([4.0 * k1, 6.0 * k2, 4.0 * k3, k4], axis=0))
    return jnp.concatenate([hi, hi, lo], axis=1)


def mix(lhs, cells):
    lev, _, n = cells.shape
    hi, lo = split(cells.reshape(lev * 8, n))
    out = dot(lhs, jnp.concatenate([hi, lo, hi], axis=0))
    return out.reshape(lhs.shape[0] // (lev * 8), lev, 8, n)


BANDS = ((1,), (1, 1), (3, 2, 1), (7, 6, 3, 1), (19, 16, 10, 4, 1))
CHOOSE = ((1,), (1, 1), (1, 2, 1), (1, 3, 3, 1), (1, 4, 6, 4, 1))


def strip_operator(out_ref, levels, rows):
    lev = levels.shape[0]
    ext = rows + 8
    size = lev * rows
    power = [None, vertical * levels]
    for n in range(2, STEPS + 1):
        power.append(exact_dot(power[n - 1], power[1]))
    spread = (
        lax.broadcasted_iota(I32, (size, lev), 0) // rows == lax.broadcasted_iota(I32, (size, lev), 1)
    ).astype(F32)
    tall = [None] + [exact_dot(spread, p) for p in power[1:]]
    base = 0
    for per, first, times in ((rows, 0, 2), (8, rows, 1)):
        n_col = lev * per
        spread_c = (
            lax.broadcasted_iota(I32, (lev, n_col), 1) // per == lax.broadcasted_iota(I32, (lev, n_col), 0)
        ).astype(F32)
        wide = [exact_dot(spread, spread_c)] + [exact_dot(p, spread_c) for p in tall[1:]]
        x = lax.broadcasted_iota(I32, (size, n_col), 0) % rows
        x_in = lax.broadcasted_iota(I32, (size, n_col), 1) % per + first
        apart = jnp.abs(x_in - x)
        apart = jnp.minimum(apart, ext - apart)
        band = []
        for m in range(STEPS + 1):
            value = jnp.zeros((size, n_col), F32)
            for d in range(m + 1):
                value = jnp.where(apart == d, diffuse ** m * BANDS[m][d], value)
            band.append(value)
        for k in range(STEPS):
            n = STEPS - k
            value = jnp.zeros((size, n_col), F32)
            for i in range(n + 1):
                value = value + CHOOSE[n][i] * band[n - i] * wide[i]
            hi, lo = split(CHOOSE[STEPS][k] * diffuse ** k * value)
            at = pl.ds(k * size, size)
            for copy in range(times):
                out_ref[at, base + copy * n_col:base + (copy + 1) * n_col] = hi
            out_ref[at, base + times * n_col:base + (times + 1) * n_col] = lo
        base = base + (times + 1) * n_col


def tile_map(tiles, count, owner, block, source, span, obl, orow, nch, rows, chunks):
    live = lax.broadcasted_iota(I32, (1, tiles), 1) < count
    dest = (owner & 1) * span + (owner >> 1) * obl
    dest = dest + (block & (nch - 1)) * orow + (block >> (nch.bit_length() - 1))
    dest = jnp.where(live, dest, -1)
    place = (source & (chunks - 1)) * rows + (source >> (chunks.bit_length() - 1))
    place = jnp.where(live, place, -1)
    eye = lax.broadcasted_iota(I32, (tiles, tiles), 0) == lax.broadcasted_iota(I32, (tiles, tiles), 1)

    def column(x):
        return jnp.sum(jnp.where(eye, x.astype(F32), 0.0), axis=1, keepdims=True).astype(I32)

    return dest, place, column(dest), column(place)


def pack_pairs(cells):
    n2, _, n = cells.shape
    pairs = cells.reshape(n2 // 2, 2, 8, n)
    a, b = pairs[:, 0], pairs[:, 1]
    upper = lax.broadcasted_iota(I32, a.shape, 1) < 4
    top = jnp.where(upper, a, pltpu.roll(b, 4, 1))
    bottom = jnp.where(upper, pltpu.roll(a, 4, 1), b)
    return top, bottom


def halo_pair(high, low):
    upper = lax.broadcasted_iota(I32, high.shape, 0) < 4
    first = jnp.where(upper, high, pltpu.roll(low, 4, 0))
    second = jnp.where(upper, pltpu.roll(high, 4, 0), low)
    return first, second


def spread_groups(rows):
    which = lax.broadcasted_iota(I32, rows.shape, 0) % 8
    return jnp.concatenate([jnp.where(which == t, rows, 0.0).astype(BF16) for t in range(8)], axis=1)


def body(
    grid_shape,
    w_hbm, atm_hbm, ocean_ref, alev_ref, olev_ref, owner_ref, block_ref, source_ref, count_ref,
    out_hbm, oout_ref, flux_ref,
    w, atm, res, halo_src, halo_dst, halo, terms,
    o_src, o_dst, os_src, os_dst, om_src, om_dst, oext, oterms, o_lhs, a_lhs,
    tiles_f, contrib, acc, acc_in, send2, inbox, flux_all,
    w_sem, atm_sem, out_sem, h_send, h_recv, o_send, o_recv, p1_sem, p2_send, p2_recv, p3_send, p3_recv, p4_sem,
):
    n_grp, n_dom = grid_shape
    nv, lev, rows, cols = atm.shape
    tiles = w.shape[0]
    chunks = cols // 128
    half = n_dom // 2
    nc = n_grp * half
    obl = send2.shape[0] // nc
    orow = ocean_ref.shape[2]
    ocol = ocean_ref.shape[3]
    g, j = lax.axis_index("grp"), lax.axis_index("dom")
    me = g * n_dom + j
    core = lax.rem(j, 2)
    chip = g * half + j // 2
    total = n_grp * n_dom

    def flat(d):
        return (d // n_dom, lax.rem(d, n_dom))

    def peer(k):
        c = lax.rem(chip + k, nc)
        return c, (c // half, lax.rem(c, half) * 2 + core)

    right, left = flat(lax.rem(me + 1, total)), flat(lax.rem(me + total - 1, total))
    partner = (g, j + 1 - 2 * core)
    up, down = (g, lax.rem(j + n_dom - 1, n_dom)), (g, lax.rem(j + 1, n_dom))
    side, side_up, side_down = (1 - g, j), (1 - g, up[1]), (1 - g, down[1])

    parts = w_sem.shape[0]
    per = tiles // parts

    def w_copy(c):
        span = pl.ds(c * per, per)
        return pltpu.make_async_copy(w_hbm.at[span], w.at[span], w_sem.at[c])

    def atm_copy(v):
        return pltpu.make_async_copy(atm_hbm.at[v], atm.at[v], atm_sem.at[v])

    for v in range(nv):
        atm_copy(v).start()
    for c in range(parts):
        w_copy(c).start()

    barrier = pltpu.get_barrier_semaphore()
    for who in (right, left, up, down, side, side_up, side_down):
        pl.semaphore_signal(barrier, inc=1, device_id=who, device_id_type=MESH)

    def greet(k, carry):
        pl.semaphore_signal(barrier, inc=1, device_id=peer(k)[1], device_id_type=MESH)
        return carry

    lax.fori_loop(1, nc, greet, 0)

    ocean = ocean_ref[...].reshape(nv * lev, orow, ocol)
    otop, obottom = pack_pairs(ocean)
    pairs = nv * lev // 2
    o_src[0] = otop.reshape(pairs * 8, ocol).astype(BF16)
    o_src[1] = obottom.reshape(pairs * 8, ocol).astype(BF16)

    def edge(x):
        return jnp.where(g == 0, x[..., ocol - 128:], x[..., :128])

    os_src[0] = edge(otop).reshape(pairs * 8, 128).astype(BF16)
    os_src[1] = edge(obottom).reshape(pairs * 8, 128).astype(BF16)
    om_src[...] = edge(ocean).reshape(nv * lev * 8, 128).astype(BF16)

    pl.semaphore_wait(barrier, 7 + nc - 1)

    def remote(src, dst, ssem, rsem, who):
        return pltpu.make_async_remote_copy(
            src_ref=src, dst_ref=dst, send_sem=ssem, recv_sem=rsem, device_id=who, device_id_type=MESH
        )

    o_copies = [
        remote(o_src.at[0], o_dst.at[0], o_send.at[0], o_recv.at[0], up),
        remote(o_src.at[1], o_dst.at[1], o_send.at[1], o_recv.at[1], down),
        remote(os_src.at[0], os_dst.at[0], o_send.at[2], o_recv.at[2], side_up),
        remote(os_src.at[1], os_dst.at[1], o_send.at[3], o_recv.at[3], side_down),
        remote(om_src, om_dst, o_send.at[4], o_recv.at[4], side),
    ]
    for copy in o_copies:
        copy.start()

    for v in range(nv):
        atm_copy(v).wait()
    h_copies = [
        remote(halo_src.at[0], halo_dst.at[0], h_send.at[0], h_recv.at[0], left),
        remote(halo_src.at[1], halo_dst.at[1], h_send.at[1], h_recv.at[1], right),
    ]

    def pack_halo(i, carry):
        v, pair = i // (lev // 4), lax.rem(i, lev // 4) * 4
        top, _ = pack_pairs(atm[v, pl.ds(pair, 4), 0:8, :])
        _, bottom = pack_pairs(atm[v, pl.ds(pair, 4), rows - 8:rows, :])
        span = pl.ds(pl.multiple_of(i * 16, 16), 16)
        halo_src[0, span, :] = top.reshape(16, cols).astype(BF16)
        halo_src[1, span, :] = bottom.reshape(16, cols).astype(BF16)
        return carry

    lax.fori_loop(0, nv * lev // 4, pack_halo, 0)
    for copy in h_copies:
        copy.start()

    nch = ocol // 128
    span = nc * obl
    dest, _, _, place_col = tile_map(
        tiles, count_ref[0], owner_ref[...], block_ref[...], source_ref[...], span, obl, orow, nch, rows, chunks
    )
    nblk = chunks * rows
    pick = (lax.broadcasted_iota(I32, (tiles, nblk), 1) == place_col).astype(F32).astype(BF16)

    def as_blocks(v):
        field = atm[v, 0]
        return jnp.concatenate([field[:, c * 128:(c + 1) * 128] for c in range(chunks)], axis=0)

    surface = jnp.concatenate([as_blocks(v) for v in range(nv)], axis=1).astype(BF16)

    def tile_rows(values):
        values = values.reshape(tiles // 8, 8, nv * 128)
        tiles_f[...] = jnp.concatenate([values[:, :, v * 128:(v + 1) * 128] for v in range(nv)], axis=1)

    tile_rows(dot(pick, surface))

    def keep(i, out):
        for h in range(2):
            part = out[h * 16:(h + 1) * 16, h * 128:(h + 1) * 128]
            at = pl.ds(pl.multiple_of(i * 16 + h * 8, 8), 8)
            contrib[at, 0:128] = part[0:8]
            contrib[at, 128:256] = part[8:16]

    def forward(c, carry):
        w_copy(c).wait()
        for s in range(per // 16):
            i = c * (per // 16) + s
            lhs = jnp.concatenate([spread_groups(tiles_f[2 * i]), spread_groups(tiles_f[2 * i + 1])], axis=0)
            both = w[pl.ds(i * 16, 16)].reshape(2, 1024, 128)
            keep(i, dot(lhs, jnp.concatenate([both[0], both[1]], axis=1)))
        return carry

    lax.fori_loop(0, parts, forward, 0)

    chi, clo = split(contrib[...])
    for h in range(2):
        hot = (lax.broadcasted_iota(I32, (span, tiles), 0) + h * span == dest).astype(F32).astype(BF16)
        acc[h] = dot(hot, chi) + dot(hot, clo)
    p1 = remote(acc.at[1 - core], acc_in, p1_sem.at[0], p1_sem.at[1], partner)
    p1.start()
    o_lhs[...] = level_terms(olev_ref[...])
    strip_operator(a_lhs, alev_ref[...], rows)
    p1.wait_recv()
    own = acc[core] + acc_in[...]
    send2[...] = own.astype(BF16)

    def slot(ref, c):
        return ref.at[pl.ds(pl.multiple_of(c * obl, obl), obl)]

    def p2(k):
        c, who = peer(k)
        return remote(slot(send2, c), slot(inbox, chip), p2_send.at[c], p2_recv.at[chip], who)

    def p2_in(k):
        c, who = peer(k)
        return remote(slot(send2, c), slot(inbox, c), p2_send.at[c], p2_recv.at[c], who)

    def loop(f):
        def step(k, carry):
            f(k)
            return carry

        lax.fori_loop(1, nc, step, 0)

    loop(lambda k: p2(k).start())
    for copy in o_copies:
        copy.wait_recv()
    for v in range(nv):
        m = nv * lev // 2 // nv
        top = jnp.concatenate([o_dst[0], os_dst[0]], axis=1).astype(F32).reshape(pairs, 8, ocol + 128)
        bottom = jnp.concatenate([o_dst[1], os_dst[1]], axis=1).astype(F32).reshape(pairs, 8, ocol + 128)
        beside = om_dst[...].astype(F32).reshape(nv, lev, 8, 128)
        oext[:, 0:8, 0:ocol] = ocean_ref[v]
        oext[:, 0:8, ocol:] = beside[v]
        for q in range(m):
            first, second = halo_pair(top[v * m + q], bottom[v * m + q])
            oext[2 * q, 8:16, :] = first
            oext[2 * q + 1, 8:16, :] = second
        for t in range(2):
            oterms[:, :, t * 8:(t + 1) * 8, :] = mix(o_lhs[...], oext[:, t * 8:(t + 1) * 8, :])
        shape = (16, ocol + 128)
        r_at, c_at = lax.broadcasted_iota(I32, shape, 0), lax.broadcasted_iota(I32, shape, 1)
        no_up = (r_at == 0) & (j == 0)
        no_down = (r_at == 7) & (j == n_dom - 1)
        no_left = (c_at == 0) & (g == 0)
        no_right = (c_at == ocol - 1) & (g == n_grp - 1)

        def ocean_level(l, carry):
            r = oext[l]
            for k in range(STEPS):
                total4 = jnp.where(no_up, 0.0, pltpu.roll(r, 1, 0)) + jnp.where(no_down, 0.0, pltpu.roll(r, 15, 0))
                total4 = total4 + jnp.where(no_left, 0.0, pltpu.roll(r, 1, 1))
                total4 = total4 + jnp.where(no_right, 0.0, pltpu.roll(r, ocol + 127, 1))
                r = diffuse * (r + total4) + oterms[k, l]
            oout_ref[v, l] = r[0:8, 0:ocol]
            return carry

        lax.fori_loop(0, lev, ocean_level, 0)
    mine = pl.ds(pl.multiple_of(chip * obl, obl), obl)
    loop(lambda k: p2_in(k).wait_recv())
    inbox[mine, :] = send2[mine, :]
    received = jnp.sum(inbox[...].astype(F32).reshape(nc, obl, nv * 128), axis=0)
    osurf = [
        jnp.concatenate([ocean_ref[v, 0, :, c * 128:(c + 1) * 128] for c in range(nch)], axis=0) for v in range(nv)
    ]
    flux = received - jnp.concatenate(osurf, axis=1)
    flux_all[core, mine, :] = flux.astype(BF16)

    def p3(k):
        c, who = peer(k)
        return remote(slot(flux_all.at[core], chip), slot(flux_all.at[core], chip), p3_send.at[c], p3_recv.at[chip], who)

    def p3_in(k):
        c, who = peer(k)
        return remote(slot(flux_all.at[core], c), slot(flux_all.at[core], c), p3_send.at[c], p3_recv.at[c], who)

    loop(lambda k: p3(k).start())

    for v in range(nv):
        field = jnp.concatenate([flux[c * 8:(c + 1) * 8, v * 128:(v + 1) * 128] for c in range(nch)], axis=1)
        oout_ref[v, 0] = oout_ref[v, 0] + couple * field

    for copy in h_copies:
        copy.wait_recv()
    zeros = jnp.zeros((rows, 128), F32)
    width = 512

    def out_copy(v):
        return pltpu.make_async_copy(res.at[v], out_hbm.at[v], out_sem.at[v])

    def along_y(r):
        padded = jnp.concatenate([r, zeros], axis=1)
        return pltpu.roll(padded, 1, 1)[:, :cols] + pltpu.roll(padded, cols + 127, 1)[:, :cols]

    p4 = remote(flux_all.at[core], flux_all.at[core], p4_sem.at[0], p4_sem.at[1], partner)
    p4_in = remote(flux_all.at[1 - core], flux_all.at[1 - core], p4_sem.at[0], p4_sem.at[1], partner)

    for v in range(nv):
        def unpack(i, carry):
            at = pl.ds(pl.multiple_of((v * lev // 4 + i) * 16, 16), 16)
            high, low = halo_dst[0, at, :].astype(F32), halo_dst[1, at, :].astype(F32)
            for q in range(2):
                first, second = halo_pair(high[q * 8:(q + 1) * 8], low[q * 8:(q + 1) * 8])
                halo[4 * i + 2 * q] = first
                halo[4 * i + 2 * q + 1] = second
            return carry

        lax.fori_loop(0, lev // 4, unpack, 0)

        def along_levels(c, carry):
            at = pl.ds(pl.multiple_of(c * width, width), width)
            hi, lo = split(atm[v, :, :, at].reshape(lev * rows, width))
            beyond = halo[:, :, at].reshape(lev * 8, width).astype(BF16)
            out = dot(a_lhs[...], jnp.concatenate([hi, lo, hi, beyond, beyond], axis=0))
            terms[:, :, :, at] = out.reshape(STEPS, lev, rows, width)
            return carry

        lax.fori_loop(0, cols // width, along_levels, 0)

        def atm_level(l, carry):
            r = diffuse ** STEPS * atm[v, l]
            for k in range(STEPS - 1, -1, -1):
                r = terms[k, l] + along_y(r)
            res[v, l] = r
            return carry

        lax.fori_loop(0, lev, atm_level, 0)
        out_copy(v).start()
        if v == 0:
            loop(lambda k: p3_in(k).wait_recv())
            p4.start()

    p4_in.wait_recv()
    flux_ref[...] = flux_all[...].reshape(2 * span, nv * 128)
    for copy in o_copies + h_copies + [p1, p4]:
        copy.wait_send()
    loop(lambda k: p2(k).wait_send())
    loop(lambda k: p3(k).wait_send())
    for v in range(nv):
        out_copy(v).wait()


def back_body(
    obl, orow, nch,
    w_hbm, pre_hbm, opre_hbm, flux_ref, owner_ref, block_ref, source_ref, count_ref,
    out_hbm, oout_hbm,
    w, pre, opre, acc, contrib, ret,
    w_sem, in_sem, out_sem, o_sem,
):
    nv, lev, rows, cols = pre.shape
    tiles = w.shape[0]
    chunks = cols // 128
    span = flux_ref.shape[0] // 2
    half = w_sem.shape[0]
    per = tiles // half

    def w_copy(c):
        at = pl.ds(c * per, per)
        return pltpu.make_async_copy(w_hbm.at[at], w.at[at], w_sem.at[c])

    def first_in(v):
        return pltpu.make_async_copy(pre_hbm.at[v, 0], pre.at[v, 0], in_sem.at[v, 0])

    def rest_in(v):
        at = pl.ds(1, lev - 1)
        return pltpu.make_async_copy(pre_hbm.at[v, at], pre.at[v, at], in_sem.at[v, 1])

    def first_out(v):
        return pltpu.make_async_copy(pre.at[v, 0], out_hbm.at[v, 0], out_sem.at[v, 0])

    def rest_out(v):
        at = pl.ds(1, lev - 1)
        return pltpu.make_async_copy(pre.at[v, at], out_hbm.at[v, at], out_sem.at[v, 1])

    o_in = pltpu.make_async_copy(opre_hbm, opre, o_sem.at[0])
    o_out = pltpu.make_async_copy(opre, oout_hbm, o_sem.at[1])
    for c in range(half):
        w_copy(c).start()
    o_in.start()
    for v in range(nv):
        rest_in(v).start()
        first_in(v).start()

    _, place, dest_col, _ = tile_map(
        tiles, count_ref[0], owner_ref[...], block_ref[...], source_ref[...], span, obl, orow, nch, rows, chunks
    )
    hot = (lax.broadcasted_iota(I32, (tiles, 2 * span), 1) == dest_col).astype(F32).astype(BF16)
    values = dot(hot, flux_ref[...])
    column = lax.broadcasted_iota(I32, (128, 256), 1) % 64
    step = 4
    blank = jnp.zeros((128, 128), BF16)
    for q in range(tiles // 128):
        groups = []
        for h in range(2):
            at = q * 128 + h * 64
            both = jnp.concatenate([values[at:at + 64, v * 128:(v + 1) * 128] for v in range(nv)], axis=0)
            groups.append(both.T.astype(BF16))
        rhs = jnp.concatenate(
            [
                jnp.concatenate([groups[0], blank], axis=1),
                jnp.concatenate([blank, groups[1]], axis=1),
            ],
            axis=0,
        )
        for c in range(q * half * 128 // tiles, (q + 1) * half * 128 // tiles):
            w_copy(c).wait()
        acc[...] = jnp.zeros((128, 256), F32)

        def some(i, carry):
            first = w[pl.ds(q * 128 + i * step, step)].reshape(step * 128, 128)
            second = w[pl.ds(q * 128 + 64 + i * step, step)].reshape(step * 128, 128)
            out = dot(jnp.concatenate([first, second], axis=1), rhs)
            total = acc[...]
            for t in range(step):
                total = jnp.where(column == i * step + t, out[t * 128:(t + 1) * 128], total)
            acc[...] = total
            return carry

        lax.fori_loop(0, 64 // step, some, 0)
        turned = acc[...].T
        for h in range(2):
            for v in range(nv):
                at = h * 128 + v * 64
                contrib[q * 128 + h * 64:q * 128 + (h + 1) * 64, v * 128:(v + 1) * 128] = turned[at:at + 64]
        if q == 0:
            o_in.wait()
            o_out.start()
            for v in range(nv):
                rest_in(v).wait()
                rest_out(v).start()

    bhi, blo = split(contrib[...])
    to_block = (lax.broadcasted_iota(I32, (chunks * rows, tiles), 0) == place).astype(F32).astype(BF16)
    ret[...] = dot(to_block, bhi) + dot(to_block, blo)
    for v in range(nv):
        first_in(v).wait()
        field = jnp.concatenate(
            [ret[c * rows:(c + 1) * rows, v * 128:(v + 1) * 128] for c in range(chunks)], axis=1
        )
        pre[v, 0] = pre[v, 0] - couple * field
        first_out(v).start()
    o_out.wait()
    for v in range(nv):
        rest_out(v).wait()
        first_out(v).wait()


def solution(mesh):
    n_grp, n_dom = mesh.shape["grp"], mesh.shape["dom"]
    nc = n_grp * n_dom // 2

    def per_device(
        atm_state, ocean_state, atm_levels, ocean_levels, tile_weight, tile_owner, tile_block, tile_source, tile_count
    ):
        nv, lev, rows, cols = atm_state.shape
        tiles = tile_weight.shape[0]
        orow, ocol = ocean_state.shape[2:]
        obl = orow * ocol // 128
        pairs = nv * lev // 2
        lanes = nv * 128
        dma = pltpu.SemaphoreType.DMA
        vmem = pl.BlockSpec(memory_space=pltpu.VMEM)
        hbm = pl.BlockSpec(memory_space=pl.ANY)
        tile_args = (
            tile_owner.reshape(1, tiles), tile_block.reshape(1, tiles), tile_source.reshape(1, tiles), tile_count
        )
        smem = pl.BlockSpec(memory_space=pltpu.SMEM)
        span = nc * obl
        atm_pre, ocean_pre, flux = pl.pallas_call(
            functools.partial(body, (n_grp, n_dom)),
            out_shape=(
                jax.ShapeDtypeStruct(atm_state.shape, F32),
                jax.ShapeDtypeStruct(ocean_state.shape, F32),
                jax.ShapeDtypeStruct((2 * span, lanes), BF16),
            ),
            in_specs=[hbm, hbm, vmem, vmem, vmem, vmem, vmem, vmem, smem],
            out_specs=(hbm, vmem, vmem),
            scratch_shapes=[
                pltpu.VMEM(tile_weight.shape, BF16),
                pltpu.VMEM(atm_state.shape, F32),
                pltpu.VMEM(atm_state.shape, F32),
                pltpu.VMEM((2, pairs * 8, cols), BF16),
                pltpu.VMEM((2, pairs * 8, cols), BF16),
                pltpu.VMEM((lev, 8, cols), F32),
                pltpu.VMEM((STEPS, lev, rows, cols), F32),
                pltpu.VMEM((2, pairs * 8, ocol), BF16),
                pltpu.VMEM((2, pairs * 8, ocol), BF16),
                pltpu.VMEM((2, pairs * 8, 128), BF16),
                pltpu.VMEM((2, pairs * 8, 128), BF16),
                pltpu.VMEM((nv * lev * 8, 128), BF16),
                pltpu.VMEM((nv * lev * 8, 128), BF16),
                pltpu.VMEM((lev, 16, ocol + 128), F32),
                pltpu.VMEM((STEPS, lev, 16, ocol + 128), F32),
                pltpu.VMEM((STEPS * lev * 8, 3 * lev * 8), BF16),
                pltpu.VMEM((STEPS * lev * rows, 3 * lev * rows + 2 * lev * 8), BF16),
                pltpu.VMEM((tiles // 8, 8 * nv, 128), F32),
                pltpu.VMEM((tiles, lanes), F32),
                pltpu.VMEM((2, nc * obl, lanes), F32),
                pltpu.VMEM((nc * obl, lanes), F32),
                pltpu.VMEM((nc * obl, lanes), BF16),
                pltpu.VMEM((nc * obl, lanes), BF16),
                pltpu.VMEM((2, nc * obl, lanes), BF16),
                dma((8,)), dma((nv,)), dma((nv,)),
                dma((2,)), dma((2,)), dma((5,)), dma((5,)),
                dma((2,)), dma((nc,)), dma((nc,)), dma((nc,)), dma((nc,)), dma((2,)),
            ],
            compiler_params=pltpu.CompilerParams(
                collective_id=0, has_side_effects=True, vmem_limit_bytes=60 * 1024 * 1024
            ),
            cost_estimate=pl.CostEstimate(flops=8_000_000_000, bytes_accessed=17_000_000, transcendentals=0),
        )(
            tile_weight, atm_state, ocean_state, atm_levels, ocean_levels, *tile_args
        )
        return pl.pallas_call(
            functools.partial(back_body, obl, orow, ocol // 128),
            out_shape=(
                jax.ShapeDtypeStruct(atm_state.shape, F32),
                jax.ShapeDtypeStruct(ocean_state.shape, F32),
            ),
            in_specs=[hbm, hbm, hbm, vmem, vmem, vmem, vmem, smem],
            out_specs=(hbm, hbm),
            scratch_shapes=[
                pltpu.VMEM(tile_weight.shape, BF16),
                pltpu.VMEM(atm_state.shape, F32),
                pltpu.VMEM(ocean_state.shape, F32),
                pltpu.VMEM((128, 256), F32),
                pltpu.VMEM((tiles, lanes), F32),
                pltpu.VMEM((rows * cols // 128, lanes), F32),
                dma((4,)), dma((nv, 2)), dma((nv, 2)), dma((2,)),
            ],
            compiler_params=pltpu.CompilerParams(vmem_limit_bytes=40 * 1024 * 1024),
            cost_estimate=pl.CostEstimate(flops=2_000_000_000, bytes_accessed=17_000_000, transcendentals=0),
        )(tile_weight, atm_pre, ocean_pre, flux, *tile_args)

    in_specs = (
        P(None, None, ("grp", "dom"), None),
        P(None, None, "dom", "grp"),
        P(),
        P(),
        P(("grp", "dom"), None, None),
        P(("grp", "dom"), None),
        P(("grp", "dom")),
        P(("grp", "dom")),
        P(("grp", "dom")),
    )
    out_specs = (P(None, None, ("grp", "dom"), None), P(None, None, "dom", "grp"))
    return jax.shard_map(per_device, mesh=mesh, in_specs=in_specs, out_specs=out_specs, check_vma=False)
```

```python
import functools

import jax
import jax.numpy as jnp
from jax import lax
from jax.experimental import pallas as pl
from jax.experimental.pallas import tpu as pltpu
from jax.sharding import PartitionSpec as P

STEPS = 4
MESH = pl.DeviceIdType.MESH
F32, BF16, I32 = jnp.float32, jnp.bfloat16, jnp.int32

diffuse = 0.2
vertical = 0.25
couple = 0.5


def over(x, n):
    return x >> (n.bit_length() - 1)


def within(x, n):
    return x & (n - 1)


def split(x):
    hi = x.astype(BF16)
    return hi, (x - hi.astype(F32)).astype(BF16)


def dot(a, b):
    return jnp.dot(a, b, preferred_element_type=F32)


def exact_dot(a, b):
    return jnp.dot(a, b, preferred_element_type=F32, precision=lax.Precision.HIGHEST)


def level_terms(levels):
    lev = levels.shape[0]
    size = lev * 8
    spread = (
        over(lax.broadcasted_iota(I32, (size, lev), 0), 8) == lax.broadcasted_iota(I32, (size, lev), 1)
    ).astype(F32)
    spread_t = (
        over(lax.broadcasted_iota(I32, (lev, size), 1), 8) == lax.broadcasted_iota(I32, (lev, size), 0)
    ).astype(F32)
    wide = exact_dot(exact_dot(spread, vertical * levels), spread_t)
    same = within(lax.broadcasted_iota(I32, (size, size), 0) ^ lax.broadcasted_iota(I32, (size, size), 1), 8) == 0
    k1 = jnp.where(same, wide, 0.0)
    k2 = exact_dot(k1, k1)
    k3 = exact_dot(k2, k1)
    k4 = exact_dot(k2, k2)
    hi, lo = split(jnp.concatenate([4.0 * k1, 6.0 * k2, 4.0 * k3, k4], axis=0))
    return jnp.concatenate([hi, hi, lo], axis=1)


def mix(lhs, cells):
    lev, _, n = cells.shape
    hi, lo = split(cells.reshape(lev * 8, n))
    out = dot(lhs, jnp.concatenate([hi, lo, hi], axis=0))
    return out.reshape(lhs.shape[0] // (lev * 8), lev, 8, n)


BANDS = ((1,), (1, 1), (3, 2, 1), (7, 6, 3, 1), (19, 16, 10, 4, 1))
CHOOSE = ((1,), (1, 1), (1, 2, 1), (1, 3, 3, 1), (1, 4, 6, 4, 1))


def strip_operator(out_ref, levels, rows):
    lev = levels.shape[0]
    ext = rows + 8
    size = lev * rows
    power = [None, vertical * levels]
    for n in range(2, STEPS + 1):
        power.append(exact_dot(power[n - 1], power[1]))
    spread = (
        over(lax.broadcasted_iota(I32, (size, lev), 0), rows) == lax.broadcasted_iota(I32, (size, lev), 1)
    ).astype(F32)
    tall = [None] + [exact_dot(spread, p) for p in power[1:]]
    base = 0
    for per, first, times in ((rows, 0, 2), (8, rows, 1)):
        n_col = lev * per
        spread_c = (
            over(lax.broadcasted_iota(I32, (lev, n_col), 1), per) == lax.broadcasted_iota(I32, (lev, n_col), 0)
        ).astype(F32)
        wide = [exact_dot(spread, spread_c)] + [exact_dot(p, spread_c) for p in tall[1:]]
        x = within(lax.broadcasted_iota(I32, (size, n_col), 0), rows)
        x_in = within(lax.broadcasted_iota(I32, (size, n_col), 1), per) + first
        apart = jnp.abs(x_in - x)
        apart = jnp.minimum(apart, ext - apart)
        band = []
        for m in range(STEPS + 1):
            value = jnp.zeros((size, n_col), F32)
            for d in range(m + 1):
                value = jnp.where(apart == d, diffuse ** m * BANDS[m][d], value)
            band.append(value)
        for k in range(STEPS):
            n = STEPS - k
            value = jnp.zeros((size, n_col), F32)
            for i in range(n + 1):
                value = value + CHOOSE[n][i] * band[n - i] * wide[i]
            hi, lo = split(CHOOSE[STEPS][k] * diffuse ** k * value)
            at = pl.ds(k * size, size)
            for copy in range(times):
                out_ref[at, base + copy * n_col:base + (copy + 1) * n_col] = hi
            out_ref[at, base + times * n_col:base + (times + 1) * n_col] = lo
        base = base + (times + 1) * n_col


def tile_map(tiles, count, owner, block, source, span, obl, orow, nch, rows, chunks):
    live = lax.broadcasted_iota(I32, (1, tiles), 1) < count
    dest = (owner & 1) * span + (owner >> 1) * obl
    dest = dest + (block & (nch - 1)) * orow + (block >> (nch.bit_length() - 1))
    dest = jnp.where(live, dest, -1)
    place = (source & (chunks - 1)) * rows + (source >> (chunks.bit_length() - 1))
    place = jnp.where(live, place, -1)
    eye = lax.broadcasted_iota(I32, (tiles, tiles), 0) == lax.broadcasted_iota(I32, (tiles, tiles), 1)

    def column(x):
        return jnp.sum(jnp.where(eye, x.astype(F32), 0.0), axis=1, keepdims=True).astype(I32)

    return dest, place, column(dest), column(place)


def pack_pairs(cells):
    n2, _, n = cells.shape
    pairs = cells.reshape(n2 // 2, 2, 8, n)
    a, b = pairs[:, 0], pairs[:, 1]
    upper = lax.broadcasted_iota(I32, a.shape, 1) < 4
    top = jnp.where(upper, a, pltpu.roll(b, 4, 1))
    bottom = jnp.where(upper, pltpu.roll(a, 4, 1), b)
    return top, bottom


def halo_pair(high, low):
    upper = lax.broadcasted_iota(I32, high.shape, 0) < 4
    first = jnp.where(upper, high, pltpu.roll(low, 4, 0))
    second = jnp.where(upper, pltpu.roll(high, 4, 0), low)
    return first, second


def spread_groups(rows):
    which = within(lax.broadcasted_iota(I32, rows.shape, 0), 8)
    return jnp.concatenate([jnp.where(which == t, rows, 0.0).astype(BF16) for t in range(8)], axis=1)


def body(
    grid_shape,
    w_hbm, atm_hbm, ocean_ref, alev_ref, olev_ref, owner_ref, block_ref, source_ref, count_ref,
    out_hbm, oout_ref, flux_ref,
    w, atm, res, halo_src, halo_dst, halo, *more,
):
    nv = atm.shape[0]
    terms, more = more[:nv], more[nv:]
    (
        o_src, o_dst, os_src, os_dst, om_src, om_dst, oext, oterms, o_lhs, a_lhs,
        tiles_f, contrib, acc, acc_in, send2, inbox, flux_all,
        w_sem, atm_sem, out_sem, h_send, h_recv, o_send, o_recv, p1_sem, p2_send, p2_recv, p3_send, p3_recv, p4_sem,
    ) = more
    n_grp, n_dom = grid_shape
    _, lev, rows, cols = atm.shape
    tiles = w.shape[0]
    chunks = cols // 128
    half = n_dom // 2
    nc = n_grp * half
    obl = send2.shape[0] // nc
    orow = ocean_ref.shape[2]
    ocol = ocean_ref.shape[3]
    g, j = lax.axis_index("grp"), lax.axis_index("dom")
    me = g * n_dom + j
    core = lax.rem(j, 2)
    chip = g * half + j // 2
    total = n_grp * n_dom

    def flat(d):
        return (d // n_dom, lax.rem(d, n_dom))

    def peer(k):
        c = lax.rem(chip + k, nc)
        return c, (c // half, lax.rem(c, half) * 2 + core)

    right, left = flat(lax.rem(me + 1, total)), flat(lax.rem(me + total - 1, total))
    partner = (g, j + 1 - 2 * core)
    up, down = (g, lax.rem(j + n_dom - 1, n_dom)), (g, lax.rem(j + 1, n_dom))
    side, side_up, side_down = (1 - g, j), (1 - g, up[1]), (1 - g, down[1])

    parts = w_sem.shape[0]
    per = tiles // parts

    def w_copy(c):
        span = pl.ds(c * per, per)
        return pltpu.make_async_copy(w_hbm.at[span], w.at[span], w_sem.at[c])

    def atm_copy(v):
        return pltpu.make_async_copy(atm_hbm.at[v], atm.at[v], atm_sem.at[v])

    for v in range(nv):
        atm_copy(v).start()
    for c in range(parts):
        w_copy(c).start()

    barrier = pltpu.get_barrier_semaphore()
    for who in (right, left, up, down, side, side_up, side_down):
        pl.semaphore_signal(barrier, inc=1, device_id=who, device_id_type=MESH)

    def greet(k, carry):
        pl.semaphore_signal(barrier, inc=1, device_id=peer(k)[1], device_id_type=MESH)
        return carry

    lax.fori_loop(1, nc, greet, 0)

    ocean = ocean_ref[...].reshape(nv * lev, orow, ocol)
    otop, obottom = pack_pairs(ocean)
    pairs = nv * lev // 2
    o_src[0] = otop.reshape(pairs * 8, ocol).astype(BF16)
    o_src[1] = obottom.reshape(pairs * 8, ocol).astype(BF16)

    def edge(x):
        return jnp.where(g == 0, x[..., ocol - 128:], x[..., :128])

    os_src[0] = edge(otop).reshape(pairs * 8, 128).astype(BF16)
    os_src[1] = edge(obottom).reshape(pairs * 8, 128).astype(BF16)
    om_src[...] = edge(ocean).reshape(nv * lev * 8, 128).astype(BF16)

    strip_operator(a_lhs, alev_ref[...], rows)
    pl.semaphore_wait(barrier, 7 + nc - 1)

    def remote(src, dst, ssem, rsem, who):
        return pltpu.make_async_remote_copy(
            src_ref=src, dst_ref=dst, send_sem=ssem, recv_sem=rsem, device_id=who, device_id_type=MESH
        )

    o_copies = [
        remote(o_src.at[0], o_dst.at[0], o_send.at[0], o_recv.at[0], up),
        remote(o_src.at[1], o_dst.at[1], o_send.at[1], o_recv.at[1], down),
        remote(os_src.at[0], os_dst.at[0], o_send.at[2], o_recv.at[2], side_up),
        remote(os_src.at[1], os_dst.at[1], o_send.at[3], o_recv.at[3], side_down),
        remote(om_src, om_dst, o_send.at[4], o_recv.at[4], side),
    ]
    for copy in o_copies:
        copy.start()

    for v in range(nv):
        atm_copy(v).wait()
    h_copies = [
        remote(halo_src.at[0], halo_dst.at[0], h_send.at[0], h_recv.at[0], left),
        remote(halo_src.at[1], halo_dst.at[1], h_send.at[1], h_recv.at[1], right),
    ]

    def pack_halo(i, carry):
        v, pair = i // (lev // 4), lax.rem(i, lev // 4) * 4
        top, _ = pack_pairs(atm[v, pl.ds(pair, 4), 0:8, :])
        _, bottom = pack_pairs(atm[v, pl.ds(pair, 4), rows - 8:rows, :])
        span = pl.ds(pl.multiple_of(i * 16, 16), 16)
        halo_src[0, span, :] = top.reshape(16, cols).astype(BF16)
        halo_src[1, span, :] = bottom.reshape(16, cols).astype(BF16)
        return carry

    lax.fori_loop(0, nv * lev // 4, pack_halo, 0)
    for copy in h_copies:
        copy.start()

    nch = ocol // 128
    span = nc * obl
    dest, _, _, place_col = tile_map(
        tiles, count_ref[0], owner_ref[...], block_ref[...], source_ref[...], span, obl, orow, nch, rows, chunks
    )
    nblk = chunks * rows
    pick = (lax.broadcasted_iota(I32, (tiles, nblk), 1) == place_col).astype(F32).astype(BF16)

    def as_blocks(v):
        field = atm[v, 0]
        return jnp.concatenate([field[:, c * 128:(c + 1) * 128] for c in range(chunks)], axis=0)

    surface = jnp.concatenate([as_blocks(v) for v in range(nv)], axis=1).astype(BF16)

    def tile_rows(values):
        values = values.reshape(tiles // 8, 8, nv * 128)
        tiles_f[...] = jnp.concatenate([values[:, :, v * 128:(v + 1) * 128] for v in range(nv)], axis=1)

    tile_rows(dot(pick, surface))

    def keep(i, out):
        for h in range(2):
            part = out[h * 16:(h + 1) * 16, h * 128:(h + 1) * 128]
            at = pl.ds(pl.multiple_of(i * 16 + h * 8, 8), 8)
            contrib[at, 0:128] = part[0:8]
            contrib[at, 128:256] = part[8:16]

    def forward(c, carry):
        w_copy(c).wait()
        for s in range(per // 16):
            i = c * (per // 16) + s
            lhs = jnp.concatenate([spread_groups(tiles_f[2 * i]), spread_groups(tiles_f[2 * i + 1])], axis=0)
            both = w[pl.ds(i * 16, 16)].reshape(2, 1024, 128)
            keep(i, dot(lhs, jnp.concatenate([both[0], both[1]], axis=1)))
        return carry

    lax.fori_loop(0, parts, forward, 0)

    chi, clo = split(contrib[...])
    for h in range(2):
        hot = (lax.broadcasted_iota(I32, (span, tiles), 0) + h * span == dest).astype(F32).astype(BF16)
        acc[h] = dot(hot, chi) + dot(hot, clo)
    p1 = remote(acc.at[1 - core], acc_in, p1_sem.at[0], p1_sem.at[1], partner)
    p1.start()
    o_lhs[...] = level_terms(olev_ref[...])
    p1.wait_recv()
    own = acc[core] + acc_in[...]
    send2[...] = own.astype(BF16)

    def slot(ref, c):
        return ref.at[pl.ds(pl.multiple_of(c * obl, obl), obl)]

    def p2(k):
        c, who = peer(k)
        return remote(slot(send2, c), slot(inbox, chip), p2_send.at[c], p2_recv.at[chip], who)

    def p2_in(k):
        c, who = peer(k)
        return remote(slot(send2, c), slot(inbox, c), p2_send.at[c], p2_recv.at[c], who)

    def loop(f):
        def step(k, carry):
            f(k)
            return carry

        lax.fori_loop(1, nc, step, 0)

    loop(lambda k: p2(k).start())
    for copy in o_copies:
        copy.wait_recv()
    for v in range(nv):
        m = nv * lev // 2 // nv
        top = jnp.concatenate([o_dst[0], os_dst[0]], axis=1).astype(F32).reshape(pairs, 8, ocol + 128)
        bottom = jnp.concatenate([o_dst[1], os_dst[1]], axis=1).astype(F32).reshape(pairs, 8, ocol + 128)
        beside = om_dst[...].astype(F32).reshape(nv, lev, 8, 128)
        oext[:, 0:8, 0:ocol] = ocean_ref[v]
        oext[:, 0:8, ocol:] = beside[v]
        for q in range(m):
            first, second = halo_pair(top[v * m + q], bottom[v * m + q])
            oext[2 * q, 8:16, :] = first
            oext[2 * q + 1, 8:16, :] = second
        for t in range(2):
            oterms[:, :, t * 8:(t + 1) * 8, :] = mix(o_lhs[...], oext[:, t * 8:(t + 1) * 8, :])
        shape = (16, ocol + 128)
        r_at, c_at = lax.broadcasted_iota(I32, shape, 0), lax.broadcasted_iota(I32, shape, 1)
        group = 8
        no_up = (r_at == 0) & (j == 0)
        no_down = (r_at == 7) & (j == n_dom - 1)
        no_left = (c_at == 0) & (g == 0)
        no_right = (c_at == ocol - 1) & (g == n_grp - 1)

        def ocean_levels(i, carry):
            state = [oext[i * group + q] for q in range(group)]
            for k in range(STEPS):
                for q in range(group):
                    r = state[q]
                    near = jnp.where(no_up, 0.0, pltpu.roll(r, 1, 0)) + jnp.where(no_down, 0.0, pltpu.roll(r, 15, 0))
                    near = near + jnp.where(no_left, 0.0, pltpu.roll(r, 1, 1))
                    near = near + jnp.where(no_right, 0.0, pltpu.roll(r, ocol + 127, 1))
                    state[q] = diffuse * (r + near) + oterms[k, i * group + q]
            for q in range(group):
                oout_ref[v, i * group + q] = state[q][0:8, 0:ocol]
            return carry

        lax.fori_loop(0, lev // group, ocean_levels, 0)
    mine = pl.ds(pl.multiple_of(chip * obl, obl), obl)
    loop(lambda k: p2_in(k).wait_recv())
    inbox[mine, :] = send2[mine, :]
    received = jnp.sum(inbox[...].astype(F32).reshape(nc, obl, nv * 128), axis=0)
    osurf = [
        jnp.concatenate([ocean_ref[v, 0, :, c * 128:(c + 1) * 128] for c in range(nch)], axis=0) for v in range(nv)
    ]
    flux = received - jnp.concatenate(osurf, axis=1)
    flux_all[core, mine, :] = flux.astype(BF16)

    def p3(k):
        c, who = peer(k)
        return remote(slot(flux_all.at[core], chip), slot(flux_all.at[core], chip), p3_send.at[c], p3_recv.at[chip], who)

    def p3_in(k):
        c, who = peer(k)
        return remote(slot(flux_all.at[core], c), slot(flux_all.at[core], c), p3_send.at[c], p3_recv.at[c], who)

    loop(lambda k: p3(k).start())

    for v in range(nv):
        field = jnp.concatenate([flux[c * 8:(c + 1) * 8, v * 128:(v + 1) * 128] for c in range(nch)], axis=1)
        oout_ref[v, 0] = oout_ref[v, 0] + couple * field

    for copy in h_copies:
        copy.wait_recv()
    zeros = jnp.zeros((rows, 128), F32)
    width = 512

    def out_copy(v):
        return pltpu.make_async_copy(res.at[v], out_hbm.at[v], out_sem.at[v])

    def along_y(r):
        padded = jnp.concatenate([r, zeros], axis=1)
        return pltpu.roll(padded, 1, 1)[:, :cols] + pltpu.roll(padded, cols + 127, 1)[:, :cols]

    p4 = remote(flux_all.at[core], flux_all.at[core], p4_sem.at[0], p4_sem.at[1], partner)
    p4_in = remote(flux_all.at[1 - core], flux_all.at[1 - core], p4_sem.at[0], p4_sem.at[1], partner)

    def unpack(i, carry):
        at = pl.ds(pl.multiple_of(i * 16, 16), 16)
        high, low = halo_dst[0, at, :].astype(F32), halo_dst[1, at, :].astype(F32)
        for q in range(2):
            first, second = halo_pair(high[q * 8:(q + 1) * 8], low[q * 8:(q + 1) * 8])
            halo[4 * i + 2 * q] = first
            halo[4 * i + 2 * q + 1] = second
        return carry

    lax.fori_loop(0, nv * lev // 4, unpack, 0)
    pieces = cols // width
    group = lev // pieces

    def along_levels(v, c):
        at = pl.ds(pl.multiple_of(c * width, width), width)
        hi, lo = split(atm[v, :, :, at].reshape(lev * rows, width))
        beyond = halo[v * lev:(v + 1) * lev, :, at].reshape(lev * 8, width).astype(BF16)
        out = dot(a_lhs[...], jnp.concatenate([hi, lo, hi, beyond, beyond], axis=0))
        terms[v][:, :, :, at] = out.reshape(STEPS, lev, rows, width)

    def horner(v, c):
        for q in range(group):
            l = c * group + q
            r = diffuse ** STEPS * atm[v, l]
            for k in range(STEPS - 1, -1, -1):
                r = terms[v][k, l] + along_y(r)
            res[v, l] = r

    for v in range(nv + 1):
        def stage(c, carry):
            if v < nv:
                along_levels(v, c)
            if v > 0:
                horner(v - 1, c)
            return carry

        lax.fori_loop(0, pieces, stage, 0)
        if v > 0:
            out_copy(v - 1).start()
        if v == 0:
            loop(lambda k: p3_in(k).wait_recv())
            p4.start()

    p4_in.wait_recv()
    flux_ref[...] = flux_all[...].reshape(2 * span, nv * 128)
    for copy in o_copies + h_copies + [p1, p4]:
        copy.wait_send()
    loop(lambda k: p2(k).wait_send())
    loop(lambda k: p3(k).wait_send())
    for v in range(nv):
        out_copy(v).wait()


def back_body(
    obl, orow, nch,
    w_hbm, pre_hbm, opre_hbm, flux_ref, owner_ref, block_ref, source_ref, count_ref,
    out_hbm, oout_hbm,
    w, pre, opre, acc, contrib, ret,
    w_sem, in_sem, out_sem, o_sem,
):
    nv, lev, rows, cols = pre.shape
    tiles = w.shape[0]
    chunks = cols // 128
    span = flux_ref.shape[0] // 2
    half = w_sem.shape[0]
    per = tiles // half

    def w_copy(c):
        at = pl.ds(c * per, per)
        return pltpu.make_async_copy(w_hbm.at[at], w.at[at], w_sem.at[c])

    def first_in(v):
        return pltpu.make_async_copy(pre_hbm.at[v, 0], pre.at[v, 0], in_sem.at[v, 0])

    def rest_in(v):
        at = pl.ds(1, lev - 1)
        return pltpu.make_async_copy(pre_hbm.at[v, at], pre.at[v, at], in_sem.at[v, 1])

    def first_out(v):
        return pltpu.make_async_copy(pre.at[v, 0], out_hbm.at[v, 0], out_sem.at[v, 0])

    def rest_out(v):
        at = pl.ds(1, lev - 1)
        return pltpu.make_async_copy(pre.at[v, at], out_hbm.at[v, at], out_sem.at[v, 1])

    o_in = pltpu.make_async_copy(opre_hbm, opre, o_sem.at[0])
    o_out = pltpu.make_async_copy(opre, oout_hbm, o_sem.at[1])
    for c in range(half):
        w_copy(c).start()
    o_in.start()
    for v in range(nv):
        rest_in(v).start()
        first_in(v).start()

    _, place, dest_col, _ = tile_map(
        tiles, count_ref[0], owner_ref[...], block_ref[...], source_ref[...], span, obl, orow, nch, rows, chunks
    )
    hot = (lax.broadcasted_iota(I32, (tiles, 2 * span), 1) == dest_col).astype(F32).astype(BF16)
    values = dot(hot, flux_ref[...])
    column = within(lax.broadcasted_iota(I32, (128, 256), 1), 64)
    step, sub = 16, 4
    blank = jnp.zeros((128, 128), BF16)
    for q in range(tiles // 128):
        groups = []
        for h in range(2):
            at = q * 128 + h * 64
            both = jnp.concatenate([values[at:at + 64, v * 128:(v + 1) * 128] for v in range(nv)], axis=0)
            groups.append(both.T.astype(BF16))
        rhs = jnp.concatenate(
            [
                jnp.concatenate([groups[0], blank], axis=1),
                jnp.concatenate([blank, groups[1]], axis=1),
            ],
            axis=0,
        )
        for c in range(q * half * 128 // tiles, (q + 1) * half * 128 // tiles):
            w_copy(c).wait()
        acc[...] = jnp.zeros((128, 256), F32)

        def some(i, carry):
            total = acc[...]
            for s in range(0, step, sub):
                at = q * 128 + i * step + s
                first = w[pl.ds(at, sub)].reshape(sub * 128, 128)
                second = w[pl.ds(at + 64, sub)].reshape(sub * 128, 128)
                out = dot(jnp.concatenate([first, second], axis=1), rhs)
                for t in range(sub):
                    total = jnp.where(column == i * step + s + t, out[t * 128:(t + 1) * 128], total)
            acc[...] = total
            return carry

        lax.fori_loop(0, 64 // step, some, 0)
        turned = acc[...].T
        for h in range(2):
            for v in range(nv):
                at = h * 128 + v * 64
                contrib[q * 128 + h * 64:q * 128 + (h + 1) * 64, v * 128:(v + 1) * 128] = turned[at:at + 64]
        if q == 0:
            o_in.wait()
            o_out.start()
            for v in range(nv):
                rest_in(v).wait()
                rest_out(v).start()

    bhi, blo = split(contrib[...])
    to_block = (lax.broadcasted_iota(I32, (chunks * rows, tiles), 0) == place).astype(F32).astype(BF16)
    ret[...] = dot(to_block, bhi) + dot(to_block, blo)
    for v in range(nv):
        first_in(v).wait()
        field = jnp.concatenate(
            [ret[c * rows:(c + 1) * rows, v * 128:(v + 1) * 128] for c in range(chunks)], axis=1
        )
        pre[v, 0] = pre[v, 0] - couple * field
        first_out(v).start()
    o_out.wait()
    for v in range(nv):
        rest_out(v).wait()
        first_out(v).wait()


def solution(mesh):
    n_grp, n_dom = mesh.shape["grp"], mesh.shape["dom"]
    nc = n_grp * n_dom // 2

    def per_device(
        atm_state, ocean_state, atm_levels, ocean_levels, tile_weight, tile_owner, tile_block, tile_source, tile_count
    ):
        nv, lev, rows, cols = atm_state.shape
        tiles = tile_weight.shape[0]
        orow, ocol = ocean_state.shape[2:]
        obl = orow * ocol // 128
        pairs = nv * lev // 2
        lanes = nv * 128
        dma = pltpu.SemaphoreType.DMA
        vmem = pl.BlockSpec(memory_space=pltpu.VMEM)
        hbm = pl.BlockSpec(memory_space=pl.ANY)
        tile_args = (
            tile_owner.reshape(1, tiles), tile_block.reshape(1, tiles), tile_source.reshape(1, tiles), tile_count
        )
        smem = pl.BlockSpec(memory_space=pltpu.SMEM)
        span = nc * obl
        atm_pre, ocean_pre, flux = pl.pallas_call(
            functools.partial(body, (n_grp, n_dom)),
            out_shape=(
                jax.ShapeDtypeStruct(atm_state.shape, F32),
                jax.ShapeDtypeStruct(ocean_state.shape, F32),
                jax.ShapeDtypeStruct((2 * span, lanes), BF16),
            ),
            in_specs=[hbm, hbm, vmem, vmem, vmem, vmem, vmem, vmem, smem],
            out_specs=(hbm, vmem, vmem),
            scratch_shapes=[
                pltpu.VMEM(tile_weight.shape, BF16),
                pltpu.VMEM(atm_state.shape, F32),
                pltpu.VMEM(atm_state.shape, F32),
                pltpu.VMEM((2, pairs * 8, cols), BF16),
                pltpu.VMEM((2, pairs * 8, cols), BF16),
                pltpu.VMEM((nv * lev, 8, cols), F32),
                *[pltpu.VMEM((STEPS, lev, rows, cols), F32)] * nv,
                pltpu.VMEM((2, pairs * 8, ocol), BF16),
                pltpu.VMEM((2, pairs * 8, ocol), BF16),
                pltpu.VMEM((2, pairs * 8, 128), BF16),
                pltpu.VMEM((2, pairs * 8, 128), BF16),
                pltpu.VMEM((nv * lev * 8, 128), BF16),
                pltpu.VMEM((nv * lev * 8, 128), BF16),
                pltpu.VMEM((lev, 16, ocol + 128), F32),
                pltpu.VMEM((STEPS, lev, 16, ocol + 128), F32),
                pltpu.VMEM((STEPS * lev * 8, 3 * lev * 8), BF16),
                pltpu.VMEM((STEPS * lev * rows, 3 * lev * rows + 2 * lev * 8), BF16),
                pltpu.VMEM((tiles // 8, 8 * nv, 128), F32),
                pltpu.VMEM((tiles, lanes), F32),
                pltpu.VMEM((2, nc * obl, lanes), F32),
                pltpu.VMEM((nc * obl, lanes), F32),
                pltpu.VMEM((nc * obl, lanes), BF16),
                pltpu.VMEM((nc * obl, lanes), BF16),
                pltpu.VMEM((2, nc * obl, lanes), BF16),
                dma((4,)), dma((nv,)), dma((nv,)),
                dma((2,)), dma((2,)), dma((5,)), dma((5,)),
                dma((2,)), dma((nc,)), dma((nc,)), dma((nc,)), dma((nc,)), dma((2,)),
            ],
            compiler_params=pltpu.CompilerParams(
                collective_id=0, has_side_effects=True, vmem_limit_bytes=60 * 1024 * 1024
            ),
            cost_estimate=pl.CostEstimate(flops=8_000_000_000, bytes_accessed=17_000_000, transcendentals=0),
        )(
            tile_weight, atm_state, ocean_state, atm_levels, ocean_levels, *tile_args
        )
        return pl.pallas_call(
            functools.partial(back_body, obl, orow, ocol // 128),
            out_shape=(
                jax.ShapeDtypeStruct(atm_state.shape, F32),
                jax.ShapeDtypeStruct(ocean_state.shape, F32),
            ),
            in_specs=[hbm, hbm, hbm, vmem, vmem, vmem, vmem, smem],
            out_specs=(hbm, hbm),
            scratch_shapes=[
                pltpu.VMEM(tile_weight.shape, BF16),
                pltpu.VMEM(atm_state.shape, F32),
                pltpu.VMEM(ocean_state.shape, F32),
                pltpu.VMEM((128, 256), F32),
                pltpu.VMEM((tiles, lanes), F32),
                pltpu.VMEM((rows * cols // 128, lanes), F32),
                dma((4,)), dma((nv, 2)), dma((nv, 2)), dma((2,)),
            ],
            compiler_params=pltpu.CompilerParams(vmem_limit_bytes=60 * 1024 * 1024),
            cost_estimate=pl.CostEstimate(flops=2_000_000_000, bytes_accessed=17_000_000, transcendentals=0),
        )(tile_weight, atm_pre, ocean_pre, flux, *tile_args)

    in_specs = (
        P(None, None, ("grp", "dom"), None),
        P(None, None, "dom", "grp"),
        P(),
        P(),
        P(("grp", "dom"), None, None),
        P(("grp", "dom"), None),
        P(("grp", "dom")),
        P(("grp", "dom")),
        P(("grp", "dom")),
    )
    out_specs = (P(None, None, ("grp", "dom"), None), P(None, None, "dom", "grp"))
    return jax.shard_map(per_device, mesh=mesh, in_specs=in_specs, out_specs=out_specs, check_vma=False)
```

```python
import functools

import jax
import jax.numpy as jnp
from jax import lax
from jax.experimental import pallas as pl
from jax.experimental.pallas import tpu as pltpu
from jax.sharding import PartitionSpec as P

STEPS = 4
MESH = pl.DeviceIdType.MESH
F32, BF16, I32 = jnp.float32, jnp.bfloat16, jnp.int32

diffuse = 0.2
vertical = 0.25
couple = 0.5


def over(x, n):
    return x >> (n.bit_length() - 1)


def within(x, n):
    return x & (n - 1)


def split(x):
    hi = x.astype(BF16)
    return hi, (x - hi.astype(F32)).astype(BF16)


def dot(a, b):
    return jnp.dot(a, b, preferred_element_type=F32)


def exact_dot(a, b):
    return jnp.dot(a, b, preferred_element_type=F32, precision=lax.Precision.HIGHEST)


def level_terms(levels):
    lev = levels.shape[0]
    size = lev * 8
    spread = (
        over(lax.broadcasted_iota(I32, (size, lev), 0), 8) == lax.broadcasted_iota(I32, (size, lev), 1)
    ).astype(F32)
    spread_t = (
        over(lax.broadcasted_iota(I32, (lev, size), 1), 8) == lax.broadcasted_iota(I32, (lev, size), 0)
    ).astype(F32)
    wide = exact_dot(exact_dot(spread, vertical * levels), spread_t)
    same = within(lax.broadcasted_iota(I32, (size, size), 0) ^ lax.broadcasted_iota(I32, (size, size), 1), 8) == 0
    k1 = jnp.where(same, wide, 0.0)
    k2 = exact_dot(k1, k1)
    k3 = exact_dot(k2, k1)
    k4 = exact_dot(k2, k2)
    hi, lo = split(jnp.concatenate([4.0 * k1, 6.0 * k2, 4.0 * k3, k4], axis=0))
    return jnp.concatenate([hi, hi, lo], axis=1)


def mix(lhs, cells):
    lev, _, n = cells.shape
    hi, lo = split(cells.reshape(lev * 8, n))
    out = dot(lhs, jnp.concatenate([hi, lo, hi], axis=0))
    return out.reshape(lhs.shape[0] // (lev * 8), lev, 8, n)


BANDS = ((1,), (1, 1), (3, 2, 1), (7, 6, 3, 1), (19, 16, 10, 4, 1))
CHOOSE = ((1,), (1, 1), (1, 2, 1), (1, 3, 3, 1), (1, 4, 6, 4, 1))


def strip_operator(out_ref, levels, rows):
    lev = levels.shape[0]
    ext = rows + 8
    size = lev * rows
    power = [None, vertical * levels]
    for n in range(2, STEPS + 1):
        power.append(exact_dot(power[n - 1], power[1]))
    spread = (
        over(lax.broadcasted_iota(I32, (size, lev), 0), rows) == lax.broadcasted_iota(I32, (size, lev), 1)
    ).astype(F32)
    tall = [None] + [exact_dot(spread, p) for p in power[1:]]
    base = 0
    for per, first, times in ((rows, 0, 2), (8, rows, 1)):
        n_col = lev * per
        spread_c = (
            over(lax.broadcasted_iota(I32, (lev, n_col), 1), per) == lax.broadcasted_iota(I32, (lev, n_col), 0)
        ).astype(F32)
        wide = [exact_dot(spread, spread_c)] + [exact_dot(p, spread_c) for p in tall[1:]]
        x = lax.broadcasted_iota(I32, (rows, 128), 0)
        x_in = within(lax.broadcasted_iota(I32, (rows, 128), 1), per) + first
        apart = jnp.abs(x_in - x)
        apart = jnp.minimum(apart, ext - apart)
        band = []
        for m in range(STEPS + 1):
            value = jnp.zeros((rows, 128), F32)
            for d in range(m + 1):
                value = jnp.where(apart == d, diffuse ** m * BANDS[m][d], value)
            band.append(value)
        for k in range(STEPS):
            n = STEPS - k
            value = jnp.zeros((size, n_col), F32)
            for i in range(n + 1):
                part = CHOOSE[STEPS][k] * diffuse ** k * CHOOSE[n][i] * band[n - i]
                part = jnp.concatenate([part] * (n_col // 128), axis=1)
                value = value + jnp.concatenate([part] * lev, axis=0) * wide[i]
            hi, lo = split(value)
            at = pl.ds(k * size, size)
            for copy in range(times):
                out_ref[at, base + copy * n_col:base + (copy + 1) * n_col] = hi
            out_ref[at, base + times * n_col:base + (times + 1) * n_col] = lo
        base = base + (times + 1) * n_col


def tile_map(tiles, count, owner, block, source, span, obl, orow, nch, rows, chunks):
    live = lax.broadcasted_iota(I32, (1, tiles), 1) < count
    dest = (owner & 1) * span + (owner >> 1) * obl
    dest = dest + (block & (nch - 1)) * orow + (block >> (nch.bit_length() - 1))
    dest = jnp.where(live, dest, -1)
    place = (source & (chunks - 1)) * rows + (source >> (chunks.bit_length() - 1))
    place = jnp.where(live, place, -1)
    eye = lax.broadcasted_iota(I32, (tiles, tiles), 0) == lax.broadcasted_iota(I32, (tiles, tiles), 1)

    def column(x):
        return jnp.sum(jnp.where(eye, x.astype(F32), 0.0), axis=1, keepdims=True).astype(I32)

    return dest, place, column(dest), column(place)


def pack_pairs(cells):
    n2, _, n = cells.shape
    pairs = cells.reshape(n2 // 2, 2, 8, n)
    a, b = pairs[:, 0], pairs[:, 1]
    upper = lax.broadcasted_iota(I32, a.shape, 1) < 4
    top = jnp.where(upper, a, pltpu.roll(b, 4, 1))
    bottom = jnp.where(upper, pltpu.roll(a, 4, 1), b)
    return top, bottom


def halo_pair(high, low):
    upper = lax.broadcasted_iota(I32, high.shape, 0) < 4
    first = jnp.where(upper, high, pltpu.roll(low, 4, 0))
    second = jnp.where(upper, pltpu.roll(high, 4, 0), low)
    return first, second


def spread_groups(rows):
    which = within(lax.broadcasted_iota(I32, rows.shape, 0), 8)
    return jnp.concatenate([jnp.where(which == t, rows, 0.0).astype(BF16) for t in range(8)], axis=1)


def body(
    grid_shape,
    w_hbm, atm_hbm, ocean_ref, alev_ref, olev_ref, owner_ref, block_ref, source_ref, count_ref,
    out_hbm, oout_ref, flux_ref,
    w, atm, res, halo_src, halo_dst, halo, *more,
):
    nv = atm.shape[0]
    terms, more = more[:nv], more[nv:]
    (
        o_src, o_dst, os_src, os_dst, om_src, om_dst, oext, oterms, o_lhs, a_lhs,
        tiles_f, contrib, acc, acc_in, send2, inbox, flux_all,
        w_sem, atm_sem, out_sem, h_send, h_recv, o_send, o_recv, p1_sem, p2_send, p2_recv, p3_send, p3_recv, p4_sem,
    ) = more
    n_grp, n_dom = grid_shape
    _, lev, rows, cols = atm.shape
    tiles = w.shape[0]
    chunks = cols // 128
    half = n_dom // 2
    nc = n_grp * half
    obl = send2.shape[0] // nc
    orow = ocean_ref.shape[2]
    ocol = ocean_ref.shape[3]
    g, j = lax.axis_index("grp"), lax.axis_index("dom")
    me = g * n_dom + j
    core = lax.rem(j, 2)
    chip = g * half + j // 2
    total = n_grp * n_dom

    def flat(d):
        return (d // n_dom, lax.rem(d, n_dom))

    def peer(k):
        c = lax.rem(chip + k, nc)
        return c, (c // half, lax.rem(c, half) * 2 + core)

    right, left = flat(lax.rem(me + 1, total)), flat(lax.rem(me + total - 1, total))
    partner = (g, j + 1 - 2 * core)
    up, down = (g, lax.rem(j + n_dom - 1, n_dom)), (g, lax.rem(j + 1, n_dom))
    side, side_up, side_down = (1 - g, j), (1 - g, up[1]), (1 - g, down[1])

    parts = w_sem.shape[0]
    per = tiles // parts

    def w_copy(c):
        span = pl.ds(c * per, per)
        return pltpu.make_async_copy(w_hbm.at[span], w.at[span], w_sem.at[c])

    def atm_copy(v):
        return pltpu.make_async_copy(atm_hbm.at[v], atm.at[v], atm_sem.at[v])

    for v in range(nv):
        atm_copy(v).start()
    for c in range(parts):
        w_copy(c).start()

    barrier = pltpu.get_barrier_semaphore()
    for who in (right, left, up, down, side, side_up, side_down):
        pl.semaphore_signal(barrier, inc=1, device_id=who, device_id_type=MESH)

    def greet(k, carry):
        pl.semaphore_signal(barrier, inc=1, device_id=peer(k)[1], device_id_type=MESH)
        return carry

    lax.fori_loop(1, nc, greet, 0)

    ocean = ocean_ref[...].reshape(nv * lev, orow, ocol)
    otop, obottom = pack_pairs(ocean)
    pairs = nv * lev // 2
    o_src[0] = otop.reshape(pairs * 8, ocol).astype(BF16)
    o_src[1] = obottom.reshape(pairs * 8, ocol).astype(BF16)

    def edge(x):
        return jnp.where(g == 0, x[..., ocol - 128:], x[..., :128])

    os_src[0] = edge(otop).reshape(pairs * 8, 128).astype(BF16)
    os_src[1] = edge(obottom).reshape(pairs * 8, 128).astype(BF16)
    om_src[...] = edge(ocean).reshape(nv * lev * 8, 128).astype(BF16)

    o_lhs[...] = level_terms(olev_ref[...])
    pl.semaphore_wait(barrier, 7 + nc - 1)

    def remote(src, dst, ssem, rsem, who):
        return pltpu.make_async_remote_copy(
            src_ref=src, dst_ref=dst, send_sem=ssem, recv_sem=rsem, device_id=who, device_id_type=MESH
        )

    o_copies = [
        remote(o_src.at[0], o_dst.at[0], o_send.at[0], o_recv.at[0], up),
        remote(o_src.at[1], o_dst.at[1], o_send.at[1], o_recv.at[1], down),
        remote(os_src.at[0], os_dst.at[0], o_send.at[2], o_recv.at[2], side_up),
        remote(os_src.at[1], os_dst.at[1], o_send.at[3], o_recv.at[3], side_down),
        remote(om_src, om_dst, o_send.at[4], o_recv.at[4], side),
    ]
    for copy in o_copies:
        copy.start()

    for v in range(nv):
        atm_copy(v).wait()
    h_copies = [
        remote(halo_src.at[0], halo_dst.at[0], h_send.at[0], h_recv.at[0], left),
        remote(halo_src.at[1], halo_dst.at[1], h_send.at[1], h_recv.at[1], right),
    ]

    def pack_halo(i, carry):
        v, pair = i // (lev // 4), lax.rem(i, lev // 4) * 4
        top, _ = pack_pairs(atm[v, pl.ds(pair, 4), 0:8, :])
        _, bottom = pack_pairs(atm[v, pl.ds(pair, 4), rows - 8:rows, :])
        span = pl.ds(pl.multiple_of(i * 16, 16), 16)
        halo_src[0, span, :] = top.reshape(16, cols).astype(BF16)
        halo_src[1, span, :] = bottom.reshape(16, cols).astype(BF16)
        return carry

    lax.fori_loop(0, nv * lev // 4, pack_halo, 0)
    for copy in h_copies:
        copy.start()

    nch = ocol // 128
    span = nc * obl
    dest, _, _, place_col = tile_map(
        tiles, count_ref[0], owner_ref[...], block_ref[...], source_ref[...], span, obl, orow, nch, rows, chunks
    )
    nblk = chunks * rows
    pick = (lax.broadcasted_iota(I32, (tiles, nblk), 1) == place_col).astype(F32).astype(BF16)

    def as_blocks(v):
        field = atm[v, 0]
        return jnp.concatenate([field[:, c * 128:(c + 1) * 128] for c in range(chunks)], axis=0)

    surface = jnp.concatenate([as_blocks(v) for v in range(nv)], axis=1).astype(BF16)

    def tile_rows(values):
        values = values.reshape(tiles // 8, 8, nv * 128)
        tiles_f[...] = jnp.concatenate([values[:, :, v * 128:(v + 1) * 128] for v in range(nv)], axis=1)

    tile_rows(dot(pick, surface))

    def keep(i, out):
        for h in range(2):
            part = out[h * 16:(h + 1) * 16, h * 128:(h + 1) * 128]
            at = pl.ds(pl.multiple_of(i * 16 + h * 8, 8), 8)
            contrib[at, 0:128] = part[0:8]
            contrib[at, 128:256] = part[8:16]

    for copy in o_copies:
        copy.wait_recv()
    for v in range(nv):
        m = nv * lev // 2 // nv
        top = jnp.concatenate([o_dst[0], os_dst[0]], axis=1).astype(F32).reshape(pairs, 8, ocol + 128)
        bottom = jnp.concatenate([o_dst[1], os_dst[1]], axis=1).astype(F32).reshape(pairs, 8, ocol + 128)
        beside = om_dst[...].astype(F32).reshape(nv, lev, 8, 128)
        oext[v, :, 0:8, 0:ocol] = ocean_ref[v]
        oext[v, :, 0:8, ocol:] = beside[v]
        for q in range(m):
            first, second = halo_pair(top[v * m + q], bottom[v * m + q])
            oext[v, 2 * q, 8:16, :] = first
            oext[v, 2 * q + 1, 8:16, :] = second
        for t in range(2):
            oterms[v, :, :, t * 8:(t + 1) * 8, :] = mix(o_lhs[...], oext[v, :, t * 8:(t + 1) * 8, :])
    shape = (16, ocol + 128)
    r_at, c_at = lax.broadcasted_iota(I32, shape, 0), lax.broadcasted_iota(I32, shape, 1)
    no_up = (r_at == 0) & (j == 0)
    no_down = (r_at == 7) & (j == n_dom - 1)
    no_left = (c_at == 0) & (g == 0)
    no_right = (c_at == ocol - 1) & (g == n_grp - 1)
    at_once = nv * lev // parts
    per_v = lev // at_once

    def ocean_levels(c):
        v, base = c // per_v, lax.rem(c, per_v) * at_once
        state = [oext[v, base + q] for q in range(at_once)]
        for k in range(STEPS):
            for q in range(at_once):
                r = state[q]
                near = jnp.where(no_up, 0.0, pltpu.roll(r, 1, 0)) + jnp.where(no_down, 0.0, pltpu.roll(r, 15, 0))
                near = near + jnp.where(no_left, 0.0, pltpu.roll(r, 1, 1))
                near = near + jnp.where(no_right, 0.0, pltpu.roll(r, ocol + 127, 1))
                state[q] = diffuse * (r + near) + oterms[v, k, base + q]
        for q in range(at_once):
            oout_ref[v, base + q] = state[q][0:8, 0:ocol]

    def forward(c, carry):
        w_copy(c).wait()
        for s in range(per // 16):
            i = c * (per // 16) + s
            lhs = jnp.concatenate([spread_groups(tiles_f[2 * i]), spread_groups(tiles_f[2 * i + 1])], axis=0)
            both = w[pl.ds(i * 16, 16)].reshape(2, 1024, 128)
            keep(i, dot(lhs, jnp.concatenate([both[0], both[1]], axis=1)))
        ocean_levels(c)
        return carry

    lax.fori_loop(0, parts, forward, 0)

    chi, clo = split(contrib[...])
    for h in range(2):
        hot = (lax.broadcasted_iota(I32, (span, tiles), 0) + h * span == dest).astype(F32).astype(BF16)
        acc[h] = dot(hot, chi) + dot(hot, clo)
    p1 = remote(acc.at[1 - core], acc_in, p1_sem.at[0], p1_sem.at[1], partner)
    p1.start()
    strip_operator(a_lhs, alev_ref[...], rows)
    p1.wait_recv()
    own = acc[core] + acc_in[...]
    send2[...] = own.astype(BF16)

    def slot(ref, c):
        return ref.at[pl.ds(pl.multiple_of(c * obl, obl), obl)]

    def p2(k):
        c, who = peer(k)
        return remote(slot(send2, c), slot(inbox, chip), p2_send.at[c], p2_recv.at[chip], who)

    def p2_in(k):
        c, who = peer(k)
        return remote(slot(send2, c), slot(inbox, c), p2_send.at[c], p2_recv.at[c], who)

    def loop(f):
        def step(k, carry):
            f(k)
            return carry

        lax.fori_loop(1, nc, step, 0)

    loop(lambda k: p2(k).start())
    for copy in h_copies:
        copy.wait_recv()
    zeros = jnp.zeros((rows, 128), F32)
    width = 512

    def out_copy(v):
        return pltpu.make_async_copy(res.at[v], out_hbm.at[v], out_sem.at[v])

    def along_y(r):
        padded = jnp.concatenate([r, zeros], axis=1)
        return pltpu.roll(padded, 1, 1)[:, :cols] + pltpu.roll(padded, cols + 127, 1)[:, :cols]

    p4 = remote(flux_all.at[core], flux_all.at[core], p4_sem.at[0], p4_sem.at[1], partner)
    p4_in = remote(flux_all.at[1 - core], flux_all.at[1 - core], p4_sem.at[0], p4_sem.at[1], partner)

    def unpack(i, carry):
        at = pl.ds(pl.multiple_of(i * 16, 16), 16)
        high, low = halo_dst[0, at, :].astype(F32), halo_dst[1, at, :].astype(F32)
        for q in range(2):
            first, second = halo_pair(high[q * 8:(q + 1) * 8], low[q * 8:(q + 1) * 8])
            halo[4 * i + 2 * q] = first
            halo[4 * i + 2 * q + 1] = second
        return carry

    lax.fori_loop(0, nv * lev // 4, unpack, 0)
    pieces = cols // width
    group = lev // pieces

    def along_levels(v, c):
        at = pl.ds(pl.multiple_of(c * width, width), width)
        hi, lo = split(atm[v, :, :, at].reshape(lev * rows, width))
        beyond = halo[v * lev:(v + 1) * lev, :, at].reshape(lev * 8, width).astype(BF16)
        out = dot(a_lhs[...], jnp.concatenate([hi, lo, hi, beyond, beyond], axis=0))
        terms[v][:, :, :, at] = out.reshape(STEPS, lev, rows, width)

    def horner(v, c):
        for q in range(group):
            l = c * group + q
            r = diffuse ** STEPS * atm[v, l]
            for k in range(STEPS - 1, -1, -1):
                r = terms[v][k, l] + along_y(r)
            res[v, l] = r

    def stage(product, sums):
        def one(c, carry):
            if product is not None:
                along_levels(product, c)
            if sums is not None:
                horner(sums, c)
            return carry

        lax.fori_loop(0, pieces, one, 0)

    stage(0, None)
    mine = pl.ds(pl.multiple_of(chip * obl, obl), obl)
    loop(lambda k: p2_in(k).wait_recv())
    inbox[mine, :] = send2[mine, :]
    received = jnp.sum(inbox[...].astype(F32).reshape(nc, obl, nv * 128), axis=0)
    osurf = [
        jnp.concatenate([ocean_ref[v, 0, :, c * 128:(c + 1) * 128] for c in range(nch)], axis=0) for v in range(nv)
    ]
    flux = received - jnp.concatenate(osurf, axis=1)
    flux_all[core, mine, :] = flux.astype(BF16)

    def p3(k):
        c, who = peer(k)
        return remote(slot(flux_all.at[core], chip), slot(flux_all.at[core], chip), p3_send.at[c], p3_recv.at[chip], who)

    def p3_in(k):
        c, who = peer(k)
        return remote(slot(flux_all.at[core], c), slot(flux_all.at[core], c), p3_send.at[c], p3_recv.at[c], who)

    loop(lambda k: p3(k).start())

    for v in range(nv):
        field = jnp.concatenate([flux[c * 8:(c + 1) * 8, v * 128:(v + 1) * 128] for c in range(nch)], axis=1)
        oout_ref[v, 0] = oout_ref[v, 0] + couple * field

    for v in range(1, nv):
        stage(v, v - 1)
        out_copy(v - 1).start()
    loop(lambda k: p3_in(k).wait_recv())
    p4.start()
    stage(None, nv - 1)
    out_copy(nv - 1).start()
    p4_in.wait_recv()
    flux_ref[...] = flux_all[...].reshape(2 * span, nv * 128)
    for copy in o_copies + h_copies + [p1, p4]:
        copy.wait_send()
    loop(lambda k: p2(k).wait_send())
    loop(lambda k: p3(k).wait_send())
    for v in range(nv):
        out_copy(v).wait()


def back_body(
    obl, orow, nch,
    w_hbm, pre_hbm, opre_hbm, flux_ref, owner_ref, block_ref, source_ref, count_ref,
    out_hbm, oout_hbm,
    w, pre, opre, acc, contrib, ret,
    w_sem, in_sem, out_sem, o_sem,
):
    nv, lev, rows, cols = pre.shape
    tiles = w.shape[0]
    chunks = cols // 128
    span = flux_ref.shape[0] // 2
    half = w_sem.shape[0]
    per = tiles // half

    def w_copy(c):
        at = pl.ds(c * per, per)
        return pltpu.make_async_copy(w_hbm.at[at], w.at[at], w_sem.at[c])

    def first_in(v):
        return pltpu.make_async_copy(pre_hbm.at[v, 0], pre.at[v, 0], in_sem.at[v, 0])

    def rest_in(v):
        at = pl.ds(1, lev - 1)
        return pltpu.make_async_copy(pre_hbm.at[v, at], pre.at[v, at], in_sem.at[v, 1])

    def first_out(v):
        return pltpu.make_async_copy(pre.at[v, 0], out_hbm.at[v, 0], out_sem.at[v, 0])

    def rest_out(v):
        at = pl.ds(1, lev - 1)
        return pltpu.make_async_copy(pre.at[v, at], out_hbm.at[v, at], out_sem.at[v, 1])

    o_in = pltpu.make_async_copy(opre_hbm, opre, o_sem.at[0])
    o_out = pltpu.make_async_copy(opre, oout_hbm, o_sem.at[1])
    for c in range(half):
        w_copy(c).start()
    o_in.start()
    for v in range(nv):
        rest_in(v).start()
        first_in(v).start()

    _, place, dest_col, _ = tile_map(
        tiles, count_ref[0], owner_ref[...], block_ref[...], source_ref[...], span, obl, orow, nch, rows, chunks
    )
    hot = (lax.broadcasted_iota(I32, (tiles, 2 * span), 1) == dest_col).astype(F32).astype(BF16)
    values = dot(hot, flux_ref[...])
    column = within(lax.broadcasted_iota(I32, (128, 256), 1), 64)
    step, sub = 16, 4
    blank = jnp.zeros((128, 128), BF16)
    for q in range(tiles // 128):
        groups = []
        for h in range(2):
            at = q * 128 + h * 64
            both = jnp.concatenate([values[at:at + 64, v * 128:(v + 1) * 128] for v in range(nv)], axis=0)
            groups.append(both.T.astype(BF16))
        rhs = jnp.concatenate(
            [
                jnp.concatenate([groups[0], blank], axis=1),
                jnp.concatenate([blank, groups[1]], axis=1),
            ],
            axis=0,
        )
        for c in range(q * half * 128 // tiles, (q + 1) * half * 128 // tiles):
            w_copy(c).wait()
        acc[...] = jnp.zeros((128, 256), F32)

        def some(i, carry):
            total = acc[...]
            for s in range(0, step, sub):
                at = q * 128 + i * step + s
                first = w[pl.ds(at, sub)].reshape(sub * 128, 128)
                second = w[pl.ds(at + 64, sub)].reshape(sub * 128, 128)
                out = dot(jnp.concatenate([first, second], axis=1), rhs)
                for t in range(sub):
                    total = jnp.where(column == i * step + s + t, out[t * 128:(t + 1) * 128], total)
            acc[...] = total
            return carry

        lax.fori_loop(0, 64 // step, some, 0)
        turned = acc[...].T
        for h in range(2):
            for v in range(nv):
                at = h * 128 + v * 64
                contrib[q * 128 + h * 64:q * 128 + (h + 1) * 64, v * 128:(v + 1) * 128] = turned[at:at + 64]
        if q == 0:
            o_in.wait()
            o_out.start()
            for v in range(nv):
                rest_in(v).wait()
                rest_out(v).start()

    bhi, blo = split(contrib[...])
    to_block = (lax.broadcasted_iota(I32, (chunks * rows, tiles), 0) == place).astype(F32).astype(BF16)
    ret[...] = dot(to_block, bhi) + dot(to_block, blo)
    for v in range(nv):
        first_in(v).wait()
        field = jnp.concatenate(
            [ret[c * rows:(c + 1) * rows, v * 128:(v + 1) * 128] for c in range(chunks)], axis=1
        )
        pre[v, 0] = pre[v, 0] - couple * field
        first_out(v).start()
    o_out.wait()
    for v in range(nv):
        rest_out(v).wait()
        first_out(v).wait()


def solution(mesh):
    n_grp, n_dom = mesh.shape["grp"], mesh.shape["dom"]
    nc = n_grp * n_dom // 2

    def per_device(
        atm_state, ocean_state, atm_levels, ocean_levels, tile_weight, tile_owner, tile_block, tile_source, tile_count
    ):
        nv, lev, rows, cols = atm_state.shape
        tiles = tile_weight.shape[0]
        orow, ocol = ocean_state.shape[2:]
        obl = orow * ocol // 128
        pairs = nv * lev // 2
        lanes = nv * 128
        dma = pltpu.SemaphoreType.DMA
        vmem = pl.BlockSpec(memory_space=pltpu.VMEM)
        hbm = pl.BlockSpec(memory_space=pl.ANY)
        tile_args = (
            tile_owner.reshape(1, tiles), tile_block.reshape(1, tiles), tile_source.reshape(1, tiles), tile_count
        )
        smem = pl.BlockSpec(memory_space=pltpu.SMEM)
        span = nc * obl
        atm_pre, ocean_pre, flux = pl.pallas_call(
            functools.partial(body, (n_grp, n_dom)),
            out_shape=(
                jax.ShapeDtypeStruct(atm_state.shape, F32),
                jax.ShapeDtypeStruct(ocean_state.shape, F32),
                jax.ShapeDtypeStruct((2 * span, lanes), BF16),
            ),
            in_specs=[hbm, hbm, vmem, vmem, vmem, vmem, vmem, vmem, smem],
            out_specs=(hbm, vmem, vmem),
            scratch_shapes=[
                pltpu.VMEM(tile_weight.shape, BF16),
                pltpu.VMEM(atm_state.shape, F32),
                pltpu.VMEM(atm_state.shape, F32),
                pltpu.VMEM((2, pairs * 8, cols), BF16),
                pltpu.VMEM((2, pairs * 8, cols), BF16),
                pltpu.VMEM((nv * lev, 8, cols), F32),
                *[pltpu.VMEM((STEPS, lev, rows, cols), F32)] * nv,
                pltpu.VMEM((2, pairs * 8, ocol), BF16),
                pltpu.VMEM((2, pairs * 8, ocol), BF16),
                pltpu.VMEM((2, pairs * 8, 128), BF16),
                pltpu.VMEM((2, pairs * 8, 128), BF16),
                pltpu.VMEM((nv * lev * 8, 128), BF16),
                pltpu.VMEM((nv * lev * 8, 128), BF16),
                pltpu.VMEM((nv, lev, 16, ocol + 128), F32),
                pltpu.VMEM((nv, STEPS, lev, 16, ocol + 128), F32),
                pltpu.VMEM((STEPS * lev * 8, 3 * lev * 8), BF16),
                pltpu.VMEM((STEPS * lev * rows, 3 * lev * rows + 2 * lev * 8), BF16),
                pltpu.VMEM((tiles // 8, 8 * nv, 128), F32),
                pltpu.VMEM((tiles, lanes), F32),
                pltpu.VMEM((2, nc * obl, lanes), F32),
                pltpu.VMEM((nc * obl, lanes), F32),
                pltpu.VMEM((nc * obl, lanes), BF16),
                pltpu.VMEM((nc * obl, lanes), BF16),
                pltpu.VMEM((2, nc * obl, lanes), BF16),
                dma((4,)), dma((nv,)), dma((nv,)),
                dma((2,)), dma((2,)), dma((5,)), dma((5,)),
                dma((2,)), dma((nc,)), dma((nc,)), dma((nc,)), dma((nc,)), dma((2,)),
            ],
            compiler_params=pltpu.CompilerParams(
                collective_id=0, has_side_effects=True, vmem_limit_bytes=60 * 1024 * 1024
            ),
            cost_estimate=pl.CostEstimate(flops=8_000_000_000, bytes_accessed=17_000_000, transcendentals=0),
        )(
            tile_weight, atm_state, ocean_state, atm_levels, ocean_levels, *tile_args
        )
        return pl.pallas_call(
            functools.partial(back_body, obl, orow, ocol // 128),
            out_shape=(
                jax.ShapeDtypeStruct(atm_state.shape, F32),
                jax.ShapeDtypeStruct(ocean_state.shape, F32),
            ),
            in_specs=[hbm, hbm, hbm, vmem, vmem, vmem, vmem, smem],
            out_specs=(hbm, hbm),
            scratch_shapes=[
                pltpu.VMEM(tile_weight.shape, BF16),
                pltpu.VMEM(atm_state.shape, F32),
                pltpu.VMEM(ocean_state.shape, F32),
                pltpu.VMEM((128, 256), F32),
                pltpu.VMEM((tiles, lanes), F32),
                pltpu.VMEM((rows * cols // 128, lanes), F32),
                dma((4,)), dma((nv, 2)), dma((nv, 2)), dma((2,)),
            ],
            compiler_params=pltpu.CompilerParams(vmem_limit_bytes=60 * 1024 * 1024),
            cost_estimate=pl.CostEstimate(flops=2_000_000_000, bytes_accessed=17_000_000, transcendentals=0),
        )(tile_weight, atm_pre, ocean_pre, flux, *tile_args)

    in_specs = (
        P(None, None, ("grp", "dom"), None),
        P(None, None, "dom", "grp"),
        P(),
        P(),
        P(("grp", "dom"), None, None),
        P(("grp", "dom"), None),
        P(("grp", "dom")),
        P(("grp", "dom")),
        P(("grp", "dom")),
    )
    out_specs = (P(None, None, ("grp", "dom"), None), P(None, None, "dom", "grp"))
    return jax.shard_map(per_device, mesh=mesh, in_specs=in_specs, out_specs=out_specs, check_vma=False)
```

```python
import functools

import jax
import jax.numpy as jnp
from jax import lax
from jax.experimental import pallas as pl
from jax.experimental.pallas import tpu as pltpu
from jax.sharding import PartitionSpec as P

STEPS = 4
MESH = pl.DeviceIdType.MESH
F32, BF16, I32 = jnp.float32, jnp.bfloat16, jnp.int32

diffuse = 0.2
vertical = 0.25
couple = 0.5


def over(x, n):
    return x >> (n.bit_length() - 1)


def within(x, n):
    return x & (n - 1)


def split(x):
    hi = x.astype(BF16)
    return hi, (x - hi.astype(F32)).astype(BF16)


def dot(a, b):
    return jnp.dot(a, b, preferred_element_type=F32)


def exact_dot(a, b):
    return jnp.dot(a, b, preferred_element_type=F32, precision=lax.Precision.HIGHEST)


def level_terms(levels):
    lev = levels.shape[0]
    size = lev * 8
    spread = (
        over(lax.broadcasted_iota(I32, (size, lev), 0), 8) == lax.broadcasted_iota(I32, (size, lev), 1)
    ).astype(F32)
    spread_t = (
        over(lax.broadcasted_iota(I32, (lev, size), 1), 8) == lax.broadcasted_iota(I32, (lev, size), 0)
    ).astype(F32)
    wide = exact_dot(exact_dot(spread, vertical * levels), spread_t)
    same = within(lax.broadcasted_iota(I32, (size, size), 0) ^ lax.broadcasted_iota(I32, (size, size), 1), 8) == 0
    k1 = jnp.where(same, wide, 0.0)
    k2 = exact_dot(k1, k1)
    k3 = exact_dot(k2, k1)
    k4 = exact_dot(k2, k2)
    hi, lo = split(jnp.concatenate([4.0 * k1, 6.0 * k2, 4.0 * k3, k4], axis=0))
    return jnp.concatenate([hi, hi, lo], axis=1)


def mix(lhs, cells):
    lev, _, n = cells.shape
    hi, lo = split(cells.reshape(lev * 8, n))
    out = dot(lhs, jnp.concatenate([hi, lo, hi], axis=0))
    return out.reshape(lhs.shape[0] // (lev * 8), lev, 8, n)


BANDS = ((1,), (1, 1), (3, 2, 1), (7, 6, 3, 1), (19, 16, 10, 4, 1))
CHOOSE = ((1,), (1, 1), (1, 2, 1), (1, 3, 3, 1), (1, 4, 6, 4, 1))


def strip_operator(out_ref, levels, rows):
    lev = levels.shape[0]
    ext = rows + 8
    size = lev * rows
    power = [None, vertical * levels]
    for n in range(2, STEPS + 1):
        power.append(exact_dot(power[n - 1], power[1]))
    spread = (
        over(lax.broadcasted_iota(I32, (size, lev), 0), rows) == lax.broadcasted_iota(I32, (size, lev), 1)
    ).astype(F32)
    tall = [None] + [exact_dot(spread, p) for p in power[1:]]
    base = 0
    for per, first, times in ((rows, 0, 2), (8, rows, 1)):
        n_col = lev * per
        spread_c = (
            over(lax.broadcasted_iota(I32, (lev, n_col), 1), per) == lax.broadcasted_iota(I32, (lev, n_col), 0)
        ).astype(F32)
        wide = [exact_dot(spread, spread_c)] + [exact_dot(p, spread_c) for p in tall[1:]]
        x = lax.broadcasted_iota(I32, (rows, 128), 0)
        x_in = within(lax.broadcasted_iota(I32, (rows, 128), 1), per) + first
        apart = jnp.abs(x_in - x)
        apart = jnp.minimum(apart, ext - apart)
        band = []
        for m in range(STEPS + 1):
            value = jnp.zeros((rows, 128), F32)
            for d in range(m + 1):
                value = jnp.where(apart == d, diffuse ** m * BANDS[m][d], value)
            band.append(value)
        for k in range(STEPS):
            n = STEPS - k
            value = jnp.zeros((size, n_col), F32)
            for i in range(n + 1):
                part = CHOOSE[STEPS][k] * diffuse ** k * CHOOSE[n][i] * band[n - i]
                part = jnp.concatenate([part] * (n_col // 128), axis=1)
                value = value + jnp.concatenate([part] * lev, axis=0) * wide[i]
            hi, lo = split(value)
            at = pl.ds(k * size, size)
            for copy in range(times):
                out_ref[at, base + copy * n_col:base + (copy + 1) * n_col] = hi
            out_ref[at, base + times * n_col:base + (times + 1) * n_col] = lo
        base = base + (times + 1) * n_col


def tile_map(tiles, count, owner, block, source, span, obl, orow, nch, rows, chunks):
    live = lax.broadcasted_iota(I32, (1, tiles), 1) < count
    dest = (owner & 1) * span + (owner >> 1) * obl
    dest = dest + (block & (nch - 1)) * orow + (block >> (nch.bit_length() - 1))
    dest = jnp.where(live, dest, -1)
    place = (source & (chunks - 1)) * rows + (source >> (chunks.bit_length() - 1))
    place = jnp.where(live, place, -1)
    eye = lax.broadcasted_iota(I32, (tiles, tiles), 0) == lax.broadcasted_iota(I32, (tiles, tiles), 1)

    def column(x):
        return jnp.sum(jnp.where(eye, x.astype(F32), 0.0), axis=1, keepdims=True).astype(I32)

    return dest, place, column(dest), column(place)


def pack_pairs(cells):
    n2, _, n = cells.shape
    pairs = cells.reshape(n2 // 2, 2, 8, n)
    a, b = pairs[:, 0], pairs[:, 1]
    upper = lax.broadcasted_iota(I32, a.shape, 1) < 4
    top = jnp.where(upper, a, pltpu.roll(b, 4, 1))
    bottom = jnp.where(upper, pltpu.roll(a, 4, 1), b)
    return top, bottom


def halo_pair(high, low):
    upper = lax.broadcasted_iota(I32, high.shape, 0) < 4
    first = jnp.where(upper, high, pltpu.roll(low, 4, 0))
    second = jnp.where(upper, pltpu.roll(high, 4, 0), low)
    return first, second


def spread_groups(rows):
    which = within(lax.broadcasted_iota(I32, rows.shape, 0), 8)
    return jnp.concatenate([jnp.where(which == t, rows, 0.0).astype(BF16) for t in range(8)], axis=1)


def body(
    grid_shape,
    w_hbm, atm_hbm, ocean_ref, alev_ref, olev_ref, owner_ref, block_ref, source_ref, count_ref,
    out_hbm, oout_ref, flux_ref,
    w, atm, res, halo_src, halo_dst, halo, *more,
):
    nv = atm.shape[0]
    terms, more = more[:nv], more[nv:]
    (
        o_src, o_dst, os_src, os_dst, om_src, om_dst, oext, oterms, o_lhs, a_lhs,
        tiles_f, contrib, acc, acc_in, send2, inbox, flux_all,
        w_sem, atm_sem, out_sem, h_send, h_recv, o_send, o_recv, p1_sem, p2_send, p2_recv, p3_send, p3_recv, p4_sem,
    ) = more
    n_grp, n_dom = grid_shape
    _, lev, rows, cols = atm.shape
    tiles = w.shape[0]
    chunks = cols // 128
    half = n_dom // 2
    nc = n_grp * half
    obl = send2.shape[0] // nc
    orow = ocean_ref.shape[2]
    ocol = ocean_ref.shape[3]
    g, j = lax.axis_index("grp"), lax.axis_index("dom")
    me = g * n_dom + j
    core = lax.rem(j, 2)
    chip = g * half + j // 2
    total = n_grp * n_dom

    def flat(d):
        return (d // n_dom, lax.rem(d, n_dom))

    def peer(k):
        c = lax.rem(chip + k, nc)
        return c, (c // half, lax.rem(c, half) * 2 + core)

    right, left = flat(lax.rem(me + 1, total)), flat(lax.rem(me + total - 1, total))
    partner = (g, j + 1 - 2 * core)
    up, down = (g, lax.rem(j + n_dom - 1, n_dom)), (g, lax.rem(j + 1, n_dom))
    side, side_up, side_down = (1 - g, j), (1 - g, up[1]), (1 - g, down[1])

    parts = w_sem.shape[0]
    per = tiles // parts

    def w_copy(c):
        span = pl.ds(c * per, per)
        return pltpu.make_async_copy(w_hbm.at[span], w.at[span], w_sem.at[c])

    def atm_copy(v):
        return pltpu.make_async_copy(atm_hbm.at[v], atm.at[v], atm_sem.at[v])

    for v in range(nv):
        atm_copy(v).start()
    for c in range(parts):
        w_copy(c).start()

    barrier = pltpu.get_barrier_semaphore()
    for who in (right, left, up, down, side, side_up, side_down):
        pl.semaphore_signal(barrier, inc=1, device_id=who, device_id_type=MESH)

    def greet(k, carry):
        pl.semaphore_signal(barrier, inc=1, device_id=peer(k)[1], device_id_type=MESH)
        return carry

    lax.fori_loop(1, nc, greet, 0)

    ocean = ocean_ref[...].reshape(nv * lev, orow, ocol)
    otop, obottom = pack_pairs(ocean)
    pairs = nv * lev // 2
    o_src[0] = otop.reshape(pairs * 8, ocol).astype(BF16)
    o_src[1] = obottom.reshape(pairs * 8, ocol).astype(BF16)

    def edge(x):
        return jnp.where(g == 0, x[..., ocol - 128:], x[..., :128])

    os_src[0] = edge(otop).reshape(pairs * 8, 128).astype(BF16)
    os_src[1] = edge(obottom).reshape(pairs * 8, 128).astype(BF16)
    om_src[...] = edge(ocean).reshape(nv * lev * 8, 128).astype(BF16)

    for v in range(nv):
        atm_copy(v).wait()
    def pack_halo(i, carry):
        v, pair = i // (lev // 4), lax.rem(i, lev // 4) * 4
        top, _ = pack_pairs(atm[v, pl.ds(pair, 4), 0:8, :])
        _, bottom = pack_pairs(atm[v, pl.ds(pair, 4), rows - 8:rows, :])
        span = pl.ds(pl.multiple_of(i * 16, 16), 16)
        halo_src[0, span, :] = top.reshape(16, cols).astype(BF16)
        halo_src[1, span, :] = bottom.reshape(16, cols).astype(BF16)
        return carry

    lax.fori_loop(0, nv * lev // 4, pack_halo, 0)
    pl.semaphore_wait(barrier, 7 + nc - 1)

    def remote(src, dst, ssem, rsem, who):
        return pltpu.make_async_remote_copy(
            src_ref=src, dst_ref=dst, send_sem=ssem, recv_sem=rsem, device_id=who, device_id_type=MESH
        )

    o_copies = [
        remote(o_src.at[0], o_dst.at[0], o_send.at[0], o_recv.at[0], up),
        remote(o_src.at[1], o_dst.at[1], o_send.at[1], o_recv.at[1], down),
        remote(os_src.at[0], os_dst.at[0], o_send.at[2], o_recv.at[2], side_up),
        remote(os_src.at[1], os_dst.at[1], o_send.at[3], o_recv.at[3], side_down),
        remote(om_src, om_dst, o_send.at[4], o_recv.at[4], side),
    ]
    for copy in o_copies:
        copy.start()

    share = pairs * 8 // nv
    h_copies = []
    for v in range(nv):
        at = pl.ds(v * share, share)
        for side_at, who in ((0, left), (1, right)):
            sem = v * 2 + side_at
            h_copies.append(
                remote(halo_src.at[side_at, at], halo_dst.at[side_at, at], h_send.at[sem], h_recv.at[sem], who)
            )
    for copy in h_copies:
        copy.start()
    o_lhs[...] = level_terms(olev_ref[...])

    nch = ocol // 128
    span = nc * obl
    dest, _, _, place_col = tile_map(
        tiles, count_ref[0], owner_ref[...], block_ref[...], source_ref[...], span, obl, orow, nch, rows, chunks
    )
    nblk = chunks * rows
    pick = (lax.broadcasted_iota(I32, (tiles, nblk), 1) == place_col).astype(F32).astype(BF16)

    def as_blocks(v):
        field = atm[v, 0]
        return jnp.concatenate([field[:, c * 128:(c + 1) * 128] for c in range(chunks)], axis=0)

    surface = jnp.concatenate([as_blocks(v) for v in range(nv)], axis=1).astype(BF16)

    def tile_rows(values):
        values = values.reshape(tiles // 8, 8, nv * 128)
        tiles_f[...] = jnp.concatenate([values[:, :, v * 128:(v + 1) * 128] for v in range(nv)], axis=1)

    tile_rows(dot(pick, surface))

    def keep(i, out):
        for h in range(2):
            part = out[h * 16:(h + 1) * 16, h * 128:(h + 1) * 128]
            at = pl.ds(pl.multiple_of(i * 16 + h * 8, 8), 8)
            contrib[at, 0:128] = part[0:8]
            contrib[at, 128:256] = part[8:16]

    for copy in o_copies:
        copy.wait_recv()
    for v in range(nv):
        m = nv * lev // 2 // nv
        top = jnp.concatenate([o_dst[0], os_dst[0]], axis=1).astype(F32).reshape(pairs, 8, ocol + 128)
        bottom = jnp.concatenate([o_dst[1], os_dst[1]], axis=1).astype(F32).reshape(pairs, 8, ocol + 128)
        beside = om_dst[...].astype(F32).reshape(nv, lev, 8, 128)
        oext[v, :, 0:8, 0:ocol] = ocean_ref[v]
        oext[v, :, 0:8, ocol:] = beside[v]
        for q in range(m):
            first, second = halo_pair(top[v * m + q], bottom[v * m + q])
            oext[v, 2 * q, 8:16, :] = first
            oext[v, 2 * q + 1, 8:16, :] = second
        for t in range(2):
            oterms[v, :, :, t * 8:(t + 1) * 8, :] = mix(o_lhs[...], oext[v, :, t * 8:(t + 1) * 8, :])
    shape = (16, ocol + 128)
    r_at, c_at = lax.broadcasted_iota(I32, shape, 0), lax.broadcasted_iota(I32, shape, 1)
    no_up = (r_at == 0) & (j == 0)
    no_down = (r_at == 7) & (j == n_dom - 1)
    no_left = (c_at == 0) & (g == 0)
    no_right = (c_at == ocol - 1) & (g == n_grp - 1)
    at_once = nv * lev // parts
    per_v = lev // at_once

    def ocean_levels(c):
        v, base = c // per_v, lax.rem(c, per_v) * at_once
        state = [oext[v, base + q] for q in range(at_once)]
        for k in range(STEPS):
            for q in range(at_once):
                r = state[q]
                near = jnp.where(no_up, 0.0, pltpu.roll(r, 1, 0)) + jnp.where(no_down, 0.0, pltpu.roll(r, 15, 0))
                near = near + jnp.where(no_left, 0.0, pltpu.roll(r, 1, 1))
                near = near + jnp.where(no_right, 0.0, pltpu.roll(r, ocol + 127, 1))
                state[q] = diffuse * (r + near) + oterms[v, k, base + q]
        for q in range(at_once):
            oout_ref[v, base + q] = state[q][0:8, 0:ocol]

    def forward(c, carry):
        w_copy(c).wait()
        for s in range(per // 16):
            i = c * (per // 16) + s
            lhs = jnp.concatenate([spread_groups(tiles_f[2 * i]), spread_groups(tiles_f[2 * i + 1])], axis=0)
            both = w[pl.ds(i * 16, 16)].reshape(2, 1024, 128)
            keep(i, dot(lhs, jnp.concatenate([both[0], both[1]], axis=1)))
        ocean_levels(c)
        return carry

    lax.fori_loop(0, parts, forward, 0)

    chi, clo = split(contrib[...])
    for h in range(2):
        hot = (lax.broadcasted_iota(I32, (span, tiles), 0) + h * span == dest).astype(F32).astype(BF16)
        acc[h] = dot(hot, chi) + dot(hot, clo)
    p1 = remote(acc.at[1 - core], acc_in, p1_sem.at[0], p1_sem.at[1], partner)
    p1.start()
    strip_operator(a_lhs, alev_ref[...], rows)
    p1.wait_recv()
    own = acc[core] + acc_in[...]
    send2[...] = own.astype(BF16)

    def slot(ref, c):
        return ref.at[pl.ds(pl.multiple_of(c * obl, obl), obl)]

    def p2(k):
        c, who = peer(k)
        return remote(slot(send2, c), slot(inbox, chip), p2_send.at[c], p2_recv.at[chip], who)

    def p2_in(k):
        c, who = peer(k)
        return remote(slot(send2, c), slot(inbox, c), p2_send.at[c], p2_recv.at[c], who)

    def loop(f):
        def step(k, carry):
            f(k)
            return carry

        lax.fori_loop(1, nc, step, 0)

    loop(lambda k: p2(k).start())
    zeros = jnp.zeros((rows, 128), F32)
    width = 512

    def out_copy(v):
        return pltpu.make_async_copy(res.at[v], out_hbm.at[v], out_sem.at[v])

    def along_y(r):
        padded = jnp.concatenate([r, zeros], axis=1)
        return pltpu.roll(padded, 1, 1)[:, :cols] + pltpu.roll(padded, cols + 127, 1)[:, :cols]

    p4 = remote(flux_all.at[core], flux_all.at[core], p4_sem.at[0], p4_sem.at[1], partner)
    p4_in = remote(flux_all.at[1 - core], flux_all.at[1 - core], p4_sem.at[0], p4_sem.at[1], partner)

    def unpack(i, carry):
        at = pl.ds(pl.multiple_of(i * 16, 16), 16)
        high, low = halo_dst[0, at, :].astype(F32), halo_dst[1, at, :].astype(F32)
        for q in range(2):
            first, second = halo_pair(high[q * 8:(q + 1) * 8], low[q * 8:(q + 1) * 8])
            halo[4 * i + 2 * q] = first
            halo[4 * i + 2 * q + 1] = second
        return carry

    def halo_in(v):
        for copy in h_copies[2 * v:2 * v + 2]:
            copy.wait_recv()
        lax.fori_loop(v * lev // 4, (v + 1) * lev // 4, unpack, 0)

    pieces = cols // width
    group = lev // pieces

    def along_levels(v, c):
        at = pl.ds(pl.multiple_of(c * width, width), width)
        hi, lo = split(atm[v, :, :, at].reshape(lev * rows, width))
        beyond = halo[v * lev:(v + 1) * lev, :, at].reshape(lev * 8, width).astype(BF16)
        out = dot(a_lhs[...], jnp.concatenate([hi, lo, hi, beyond, beyond], axis=0))
        terms[v][:, :, :, at] = out.reshape(STEPS, lev, rows, width)

    def horner(v, c):
        for q in range(group):
            l = c * group + q
            r = diffuse ** STEPS * atm[v, l]
            for k in range(STEPS - 1, -1, -1):
                r = terms[v][k, l] + along_y(r)
            res[v, l] = r

    def stage(product, sums):
        def one(c, carry):
            if product is not None:
                along_levels(product, c)
            if sums is not None:
                horner(sums, c)
            return carry

        lax.fori_loop(0, pieces, one, 0)

    halo_in(0)
    stage(0, None)
    mine = pl.ds(pl.multiple_of(chip * obl, obl), obl)
    loop(lambda k: p2_in(k).wait_recv())
    inbox[mine, :] = send2[mine, :]
    received = jnp.sum(inbox[...].astype(F32).reshape(nc, obl, nv * 128), axis=0)
    osurf = [
        jnp.concatenate([ocean_ref[v, 0, :, c * 128:(c + 1) * 128] for c in range(nch)], axis=0) for v in range(nv)
    ]
    flux = received - jnp.concatenate(osurf, axis=1)
    flux_all[core, mine, :] = flux.astype(BF16)

    def p3(k):
        c, who = peer(k)
        return remote(slot(flux_all.at[core], chip), slot(flux_all.at[core], chip), p3_send.at[c], p3_recv.at[chip], who)

    def p3_in(k):
        c, who = peer(k)
        return remote(slot(flux_all.at[core], c), slot(flux_all.at[core], c), p3_send.at[c], p3_recv.at[c], who)

    loop(lambda k: p3(k).start())

    for v in range(nv):
        field = jnp.concatenate([flux[c * 8:(c + 1) * 8, v * 128:(v + 1) * 128] for c in range(nch)], axis=1)
        oout_ref[v, 0] = oout_ref[v, 0] + couple * field

    for v in range(1, nv):
        halo_in(v)
        stage(v, v - 1)
        out_copy(v - 1).start()
    loop(lambda k: p3_in(k).wait_recv())
    p4.start()
    stage(None, nv - 1)
    out_copy(nv - 1).start()
    p4_in.wait_recv()
    flux_ref[...] = flux_all[...].reshape(2 * span, nv * 128)
    for copy in o_copies + h_copies + [p1, p4]:
        copy.wait_send()
    loop(lambda k: p2(k).wait_send())
    loop(lambda k: p3(k).wait_send())
    for v in range(nv):
        out_copy(v).wait()


def back_body(
    obl, orow, nch,
    w_hbm, pre_hbm, opre_hbm, flux_ref, owner_ref, block_ref, source_ref, count_ref,
    out_hbm, oout_hbm,
    w, pre, opre, acc, contrib, ret,
    w_sem, in_sem, out_sem, o_sem,
):
    nv, lev, rows, cols = pre.shape
    tiles = w.shape[0]
    chunks = cols // 128
    span = flux_ref.shape[0] // 2
    half = w_sem.shape[0]
    per = tiles // half

    def w_copy(c):
        at = pl.ds(c * per, per)
        return pltpu.make_async_copy(w_hbm.at[at], w.at[at], w_sem.at[c])

    def first_in(v):
        return pltpu.make_async_copy(pre_hbm.at[v, 0], pre.at[v, 0], in_sem.at[v, 0])

    def rest_in(v):
        at = pl.ds(1, lev - 1)
        return pltpu.make_async_copy(pre_hbm.at[v, at], pre.at[v, at], in_sem.at[v, 1])

    def first_out(v):
        return pltpu.make_async_copy(pre.at[v, 0], out_hbm.at[v, 0], out_sem.at[v, 0])

    def rest_out(v):
        at = pl.ds(1, lev - 1)
        return pltpu.make_async_copy(pre.at[v, at], out_hbm.at[v, at], out_sem.at[v, 1])

    o_in = pltpu.make_async_copy(opre_hbm, opre, o_sem.at[0])
    o_out = pltpu.make_async_copy(opre, oout_hbm, o_sem.at[1])
    for c in range(half):
        w_copy(c).start()
    o_in.start()
    for v in range(nv):
        rest_in(v).start()
        first_in(v).start()

    _, place, dest_col, _ = tile_map(
        tiles, count_ref[0], owner_ref[...], block_ref[...], source_ref[...], span, obl, orow, nch, rows, chunks
    )
    hot = (lax.broadcasted_iota(I32, (tiles, 2 * span), 1) == dest_col).astype(F32).astype(BF16)
    values = dot(hot, flux_ref[...])
    column = within(lax.broadcasted_iota(I32, (128, 256), 1), 64)
    step, sub = 16, 4
    blank = jnp.zeros((128, 128), BF16)
    for q in range(tiles // 128):
        groups = []
        for h in range(2):
            at = q * 128 + h * 64
            both = jnp.concatenate([values[at:at + 64, v * 128:(v + 1) * 128] for v in range(nv)], axis=0)
            groups.append(both.T.astype(BF16))
        rhs = jnp.concatenate(
            [
                jnp.concatenate([groups[0], blank], axis=1),
                jnp.concatenate([blank, groups[1]], axis=1),
            ],
            axis=0,
        )
        for c in range(q * half * 128 // tiles, (q + 1) * half * 128 // tiles):
            w_copy(c).wait()
        acc[...] = jnp.zeros((128, 256), F32)

        def some(i, carry):
            total = acc[...]
            for s in range(0, step, sub):
                at = q * 128 + i * step + s
                first = w[pl.ds(at, sub)].reshape(sub * 128, 128)
                second = w[pl.ds(at + 64, sub)].reshape(sub * 128, 128)
                out = dot(jnp.concatenate([first, second], axis=1), rhs)
                for t in range(sub):
                    total = jnp.where(column == i * step + s + t, out[t * 128:(t + 1) * 128], total)
            acc[...] = total
            return carry

        lax.fori_loop(0, 64 // step, some, 0)
        turned = acc[...].T
        for h in range(2):
            for v in range(nv):
                at = h * 128 + v * 64
                contrib[q * 128 + h * 64:q * 128 + (h + 1) * 64, v * 128:(v + 1) * 128] = turned[at:at + 64]
        if q == 0:
            o_in.wait()
            o_out.start()
            for v in range(nv):
                rest_in(v).wait()
                rest_out(v).start()

    bhi, blo = split(contrib[...])
    to_block = (lax.broadcasted_iota(I32, (chunks * rows, tiles), 0) == place).astype(F32).astype(BF16)
    ret[...] = dot(to_block, bhi) + dot(to_block, blo)
    for v in range(nv):
        first_in(v).wait()
        field = jnp.concatenate(
            [ret[c * rows:(c + 1) * rows, v * 128:(v + 1) * 128] for c in range(chunks)], axis=1
        )
        pre[v, 0] = pre[v, 0] - couple * field
        first_out(v).start()
    o_out.wait()
    for v in range(nv):
        rest_out(v).wait()
        first_out(v).wait()


def solution(mesh):
    n_grp, n_dom = mesh.shape["grp"], mesh.shape["dom"]
    nc = n_grp * n_dom // 2

    def per_device(
        atm_state, ocean_state, atm_levels, ocean_levels, tile_weight, tile_owner, tile_block, tile_source, tile_count
    ):
        nv, lev, rows, cols = atm_state.shape
        tiles = tile_weight.shape[0]
        orow, ocol = ocean_state.shape[2:]
        obl = orow * ocol // 128
        pairs = nv * lev // 2
        lanes = nv * 128
        dma = pltpu.SemaphoreType.DMA
        vmem = pl.BlockSpec(memory_space=pltpu.VMEM)
        hbm = pl.BlockSpec(memory_space=pl.ANY)
        tile_args = (
            tile_owner.reshape(1, tiles), tile_block.reshape(1, tiles), tile_source.reshape(1, tiles), tile_count
        )
        smem = pl.BlockSpec(memory_space=pltpu.SMEM)
        span = nc * obl
        atm_pre, ocean_pre, flux = pl.pallas_call(
            functools.partial(body, (n_grp, n_dom)),
            out_shape=(
                jax.ShapeDtypeStruct(atm_state.shape, F32),
                jax.ShapeDtypeStruct(ocean_state.shape, F32),
                jax.ShapeDtypeStruct((2 * span, lanes), BF16),
            ),
            in_specs=[hbm, hbm, vmem, vmem, vmem, vmem, vmem, vmem, smem],
            out_specs=(hbm, vmem, vmem),
            scratch_shapes=[
                pltpu.VMEM(tile_weight.shape, BF16),
                pltpu.VMEM(atm_state.shape, F32),
                pltpu.VMEM(atm_state.shape, F32),
                pltpu.VMEM((2, pairs * 8, cols), BF16),
                pltpu.VMEM((2, pairs * 8, cols), BF16),
                pltpu.VMEM((nv * lev, 8, cols), F32),
                *[pltpu.VMEM((STEPS, lev, rows, cols), F32)] * nv,
                pltpu.VMEM((2, pairs * 8, ocol), BF16),
                pltpu.VMEM((2, pairs * 8, ocol), BF16),
                pltpu.VMEM((2, pairs * 8, 128), BF16),
                pltpu.VMEM((2, pairs * 8, 128), BF16),
                pltpu.VMEM((nv * lev * 8, 128), BF16),
                pltpu.VMEM((nv * lev * 8, 128), BF16),
                pltpu.VMEM((nv, lev, 16, ocol + 128), F32),
                pltpu.VMEM((nv, STEPS, lev, 16, ocol + 128), F32),
                pltpu.VMEM((STEPS * lev * 8, 3 * lev * 8), BF16),
                pltpu.VMEM((STEPS * lev * rows, 3 * lev * rows + 2 * lev * 8), BF16),
                pltpu.VMEM((tiles // 8, 8 * nv, 128), F32),
                pltpu.VMEM((tiles, lanes), F32),
                pltpu.VMEM((2, nc * obl, lanes), F32),
                pltpu.VMEM((nc * obl, lanes), F32),
                pltpu.VMEM((nc * obl, lanes), BF16),
                pltpu.VMEM((nc * obl, lanes), BF16),
                pltpu.VMEM((2, nc * obl, lanes), BF16),
                dma((4,)), dma((nv,)), dma((nv,)),
                dma((2 * nv,)), dma((2 * nv,)), dma((5,)), dma((5,)),
                dma((2,)), dma((nc,)), dma((nc,)), dma((nc,)), dma((nc,)), dma((2,)),
            ],
            compiler_params=pltpu.CompilerParams(
                collective_id=0, has_side_effects=True, vmem_limit_bytes=60 * 1024 * 1024
            ),
            cost_estimate=pl.CostEstimate(flops=8_000_000_000, bytes_accessed=17_000_000, transcendentals=0),
        )(
            tile_weight, atm_state, ocean_state, atm_levels, ocean_levels, *tile_args
        )
        return pl.pallas_call(
            functools.partial(back_body, obl, orow, ocol // 128),
            out_shape=(
                jax.ShapeDtypeStruct(atm_state.shape, F32),
                jax.ShapeDtypeStruct(ocean_state.shape, F32),
            ),
            in_specs=[hbm, hbm, hbm, vmem, vmem, vmem, vmem, smem],
            out_specs=(hbm, hbm),
            scratch_shapes=[
                pltpu.VMEM(tile_weight.shape, BF16),
                pltpu.VMEM(atm_state.shape, F32),
                pltpu.VMEM(ocean_state.shape, F32),
                pltpu.VMEM((128, 256), F32),
                pltpu.VMEM((tiles, lanes), F32),
                pltpu.VMEM((rows * cols // 128, lanes), F32),
                dma((4,)), dma((nv, 2)), dma((nv, 2)), dma((2,)),
            ],
            compiler_params=pltpu.CompilerParams(vmem_limit_bytes=60 * 1024 * 1024),
            cost_estimate=pl.CostEstimate(flops=2_000_000_000, bytes_accessed=17_000_000, transcendentals=0),
        )(tile_weight, atm_pre, ocean_pre, flux, *tile_args)

    in_specs = (
        P(None, None, ("grp", "dom"), None),
        P(None, None, "dom", "grp"),
        P(),
        P(),
        P(("grp", "dom"), None, None),
        P(("grp", "dom"), None),
        P(("grp", "dom")),
        P(("grp", "dom")),
        P(("grp", "dom")),
    )
    out_specs = (P(None, None, ("grp", "dom"), None), P(None, None, "dom", "grp"))
    return jax.shard_map(per_device, mesh=mesh, in_specs=in_specs, out_specs=out_specs, check_vma=False)
```

```python
import functools

import jax
import jax.numpy as jnp
from jax import lax
from jax.experimental import pallas as pl
from jax.experimental.pallas import tpu as pltpu
from jax.sharding import PartitionSpec as P

STEPS = 4
MESH = pl.DeviceIdType.MESH
F32, BF16, I32 = jnp.float32, jnp.bfloat16, jnp.int32

diffuse = 0.2
vertical = 0.25
couple = 0.5


def over(x, n):
    return x >> (n.bit_length() - 1)


def within(x, n):
    return x & (n - 1)


def split(x):
    hi = x.astype(BF16)
    return hi, (x - hi.astype(F32)).astype(BF16)


def dot(a, b):
    return jnp.dot(a, b, preferred_element_type=F32)


def exact_dot(a, b):
    return jnp.dot(a, b, preferred_element_type=F32, precision=lax.Precision.HIGHEST)


def thirds(x):
    hi, rest = x.astype(BF16), x - x.astype(BF16).astype(F32)
    mid = rest.astype(BF16)
    return [hi, mid, (rest - mid.astype(F32)).astype(BF16)]


def spread_rows(ones, x):
    return dot(jnp.concatenate([ones.astype(BF16)] * 3, axis=1), jnp.concatenate(thirds(x), axis=0))


def spread_columns(x, ones):
    return dot(jnp.concatenate(thirds(x), axis=1), jnp.concatenate([ones.astype(BF16)] * 3, axis=0))


def level_terms(levels):
    lev = levels.shape[0]
    size = lev * 8
    spread = (
        over(lax.broadcasted_iota(I32, (size, lev), 0), 8) == lax.broadcasted_iota(I32, (size, lev), 1)
    ).astype(F32)
    spread_t = (
        over(lax.broadcasted_iota(I32, (lev, size), 1), 8) == lax.broadcasted_iota(I32, (lev, size), 0)
    ).astype(F32)
    wide = spread_columns(spread_rows(spread, vertical * levels), spread_t)
    same = within(lax.broadcasted_iota(I32, (size, size), 0) ^ lax.broadcasted_iota(I32, (size, size), 1), 8) == 0
    k1 = jnp.where(same, wide, 0.0)
    k2 = exact_dot(k1, k1)
    k3 = exact_dot(k2, k1)
    k4 = exact_dot(k2, k2)
    hi, lo = split(jnp.concatenate([4.0 * k1, 6.0 * k2, 4.0 * k3, k4], axis=0))
    return jnp.concatenate([hi, hi, lo], axis=1)


def mix(lhs, cells):
    lev, _, n = cells.shape
    hi, lo = split(cells.reshape(lev * 8, n))
    out = dot(lhs, jnp.concatenate([hi, lo, hi], axis=0))
    return out.reshape(lhs.shape[0] // (lev * 8), lev, 8, n)


BANDS = ((1,), (1, 1), (3, 2, 1), (7, 6, 3, 1), (19, 16, 10, 4, 1))
CHOOSE = ((1,), (1, 1), (1, 2, 1), (1, 3, 3, 1), (1, 4, 6, 4, 1))


def strip_operator(out_ref, levels, rows):
    lev = levels.shape[0]
    ext = rows + 8
    size = lev * rows
    power = [None, vertical * levels]
    for n in range(2, STEPS + 1):
        power.append(exact_dot(power[n - 1], power[1]))
    spread = (
        over(lax.broadcasted_iota(I32, (size, lev), 0), rows) == lax.broadcasted_iota(I32, (size, lev), 1)
    ).astype(F32)
    tall = [None] + [spread_rows(spread, p) for p in power[1:]]
    base = 0
    for per, first, times in ((rows, 0, 2), (8, rows, 1)):
        n_col = lev * per
        spread_c = (
            over(lax.broadcasted_iota(I32, (lev, n_col), 1), per) == lax.broadcasted_iota(I32, (lev, n_col), 0)
        ).astype(F32)
        wide = [dot(spread.astype(BF16), spread_c.astype(BF16))] + [spread_columns(p, spread_c) for p in tall[1:]]
        x = lax.broadcasted_iota(I32, (rows, 128), 0)
        x_in = within(lax.broadcasted_iota(I32, (rows, 128), 1), per) + first
        apart = jnp.abs(x_in - x)
        apart = jnp.minimum(apart, ext - apart)
        band = []
        for m in range(STEPS + 1):
            value = jnp.zeros((rows, 128), F32)
            for d in range(m + 1):
                value = jnp.where(apart == d, diffuse ** m * BANDS[m][d], value)
            band.append(value)
        for k in range(STEPS):
            n = STEPS - k
            value = jnp.zeros((size, n_col), F32)
            for i in range(n + 1):
                part = CHOOSE[STEPS][k] * diffuse ** k * CHOOSE[n][i] * band[n - i]
                part = jnp.concatenate([part] * (n_col // 128), axis=1)
                value = value + jnp.concatenate([part] * lev, axis=0) * wide[i]
            hi, lo = split(value)
            at = pl.ds(k * size, size)
            for copy in range(times):
                out_ref[at, base + copy * n_col:base + (copy + 1) * n_col] = hi
            out_ref[at, base + times * n_col:base + (times + 1) * n_col] = lo
        base = base + (times + 1) * n_col


def tile_map(tiles, count, owner, block, source, span, obl, orow, nch, rows, chunks):
    live = lax.broadcasted_iota(I32, (1, tiles), 1) < count
    dest = (owner & 1) * span + (owner >> 1) * obl
    dest = dest + (block & (nch - 1)) * orow + (block >> (nch.bit_length() - 1))
    dest = jnp.where(live, dest, -1)
    place = (source & (chunks - 1)) * rows + (source >> (chunks.bit_length() - 1))
    place = jnp.where(live, place, -1)
    eye = lax.broadcasted_iota(I32, (tiles, tiles), 0) == lax.broadcasted_iota(I32, (tiles, tiles), 1)

    def column(x):
        return jnp.sum(jnp.where(eye, x.astype(F32), 0.0), axis=1, keepdims=True).astype(I32)

    return dest, place, column(dest), column(place)


def pack_pairs(cells):
    n2, _, n = cells.shape
    pairs = cells.reshape(n2 // 2, 2, 8, n)
    a, b = pairs[:, 0], pairs[:, 1]
    upper = lax.broadcasted_iota(I32, a.shape, 1) < 4
    top = jnp.where(upper, a, pltpu.roll(b, 4, 1))
    bottom = jnp.where(upper, pltpu.roll(a, 4, 1), b)
    return top, bottom


def halo_pair(high, low):
    upper = lax.broadcasted_iota(I32, high.shape, 0) < 4
    first = jnp.where(upper, high, pltpu.roll(low, 4, 0))
    second = jnp.where(upper, pltpu.roll(high, 4, 0), low)
    return first, second


def spread_groups(rows):
    which = within(lax.broadcasted_iota(I32, rows.shape, 0), 8)
    return jnp.concatenate([jnp.where(which == t, rows, 0.0).astype(BF16) for t in range(8)], axis=1)


def body(
    grid_shape,
    w_hbm, atm_hbm, ocean_ref, alev_ref, olev_ref, owner_ref, block_ref, source_ref, count_ref,
    out_hbm, oout_ref, flux_ref,
    w, atm, res, halo_src, halo_dst, halo, *more,
):
    nv = atm.shape[0]
    terms, more = more[:nv], more[nv:]
    (
        o_src, o_dst, os_src, os_dst, om_src, om_dst, oext, oterms, o_lhs, a_lhs,
        tiles_f, contrib, acc, acc_in, send2, inbox, flux_all,
        w_sem, atm_sem, out_sem, h_send, h_recv, o_send, o_recv, p1_sem, p2_send, p2_recv, p3_send, p3_recv, p4_sem,
    ) = more
    n_grp, n_dom = grid_shape
    _, lev, rows, cols = atm.shape
    tiles = w.shape[0]
    chunks = cols // 128
    half = n_dom // 2
    nc = n_grp * half
    obl = send2.shape[0] // nc
    orow = ocean_ref.shape[2]
    ocol = ocean_ref.shape[3]
    g, j = lax.axis_index("grp"), lax.axis_index("dom")
    me = g * n_dom + j
    core = lax.rem(j, 2)
    chip = g * half + j // 2
    total = n_grp * n_dom

    def flat(d):
        return (d // n_dom, lax.rem(d, n_dom))

    def peer(k):
        c = lax.rem(chip + k, nc)
        return c, (c // half, lax.rem(c, half) * 2 + core)

    right, left = flat(lax.rem(me + 1, total)), flat(lax.rem(me + total - 1, total))
    partner = (g, j + 1 - 2 * core)
    up, down = (g, lax.rem(j + n_dom - 1, n_dom)), (g, lax.rem(j + 1, n_dom))
    side, side_up, side_down = (1 - g, j), (1 - g, up[1]), (1 - g, down[1])

    parts = w_sem.shape[0]
    per = tiles // parts

    def w_copy(c):
        span = pl.ds(c * per, per)
        return pltpu.make_async_copy(w_hbm.at[span], w.at[span], w_sem.at[c])

    def atm_copy(v):
        return pltpu.make_async_copy(atm_hbm.at[v], atm.at[v], atm_sem.at[v])

    for v in range(nv):
        atm_copy(v).start()
    for c in range(parts):
        w_copy(c).start()

    barrier = pltpu.get_barrier_semaphore()
    for who in (right, left, up, down, side, side_up, side_down):
        pl.semaphore_signal(barrier, inc=1, device_id=who, device_id_type=MESH)

    def greet(k, carry):
        pl.semaphore_signal(barrier, inc=1, device_id=peer(k)[1], device_id_type=MESH)
        return carry

    lax.fori_loop(1, nc, greet, 0)

    ocean = ocean_ref[...].reshape(nv * lev, orow, ocol)
    otop, obottom = pack_pairs(ocean)
    pairs = nv * lev // 2
    o_src[0] = otop.reshape(pairs * 8, ocol).astype(BF16)
    o_src[1] = obottom.reshape(pairs * 8, ocol).astype(BF16)

    def edge(x):
        return jnp.where(g == 0, x[..., ocol - 128:], x[..., :128])

    os_src[0] = edge(otop).reshape(pairs * 8, 128).astype(BF16)
    os_src[1] = edge(obottom).reshape(pairs * 8, 128).astype(BF16)
    om_src[...] = edge(ocean).reshape(nv * lev * 8, 128).astype(BF16)

    o_lhs[...] = level_terms(olev_ref[...])
    pl.semaphore_wait(barrier, 7 + nc - 1)

    def remote(src, dst, ssem, rsem, who):
        return pltpu.make_async_remote_copy(
            src_ref=src, dst_ref=dst, send_sem=ssem, recv_sem=rsem, device_id=who, device_id_type=MESH
        )

    o_copies = [
        remote(o_src.at[0], o_dst.at[0], o_send.at[0], o_recv.at[0], up),
        remote(o_src.at[1], o_dst.at[1], o_send.at[1], o_recv.at[1], down),
        remote(os_src.at[0], os_dst.at[0], o_send.at[2], o_recv.at[2], side_up),
        remote(os_src.at[1], os_dst.at[1], o_send.at[3], o_recv.at[3], side_down),
        remote(om_src, om_dst, o_send.at[4], o_recv.at[4], side),
    ]
    for copy in o_copies:
        copy.start()

    for v in range(nv):
        atm_copy(v).wait()
    h_copies = [
        remote(halo_src.at[0], halo_dst.at[0], h_send.at[0], h_recv.at[0], left),
        remote(halo_src.at[1], halo_dst.at[1], h_send.at[1], h_recv.at[1], right),
    ]

    def pack_halo(i, carry):
        v, pair = i // (lev // 4), lax.rem(i, lev // 4) * 4
        top, _ = pack_pairs(atm[v, pl.ds(pair, 4), 0:8, :])
        _, bottom = pack_pairs(atm[v, pl.ds(pair, 4), rows - 8:rows, :])
        span = pl.ds(pl.multiple_of(i * 16, 16), 16)
        halo_src[0, span, :] = top.reshape(16, cols).astype(BF16)
        halo_src[1, span, :] = bottom.reshape(16, cols).astype(BF16)
        return carry

    lax.fori_loop(0, nv * lev // 4, pack_halo, 0)
    for copy in h_copies:
        copy.start()

    nch = ocol // 128
    span = nc * obl
    dest, _, _, place_col = tile_map(
        tiles, count_ref[0], owner_ref[...], block_ref[...], source_ref[...], span, obl, orow, nch, rows, chunks
    )
    nblk = chunks * rows
    pick = (lax.broadcasted_iota(I32, (tiles, nblk), 1) == place_col).astype(F32).astype(BF16)

    def as_blocks(v):
        field = atm[v, 0]
        return jnp.concatenate([field[:, c * 128:(c + 1) * 128] for c in range(chunks)], axis=0)

    surface = jnp.concatenate([as_blocks(v) for v in range(nv)], axis=1).astype(BF16)

    def tile_rows(values):
        values = values.reshape(tiles // 8, 8, nv * 128)
        tiles_f[...] = jnp.concatenate([values[:, :, v * 128:(v + 1) * 128] for v in range(nv)], axis=1)

    tile_rows(dot(pick, surface))

    def keep(i, out):
        for h in range(2):
            part = out[h * 16:(h + 1) * 16, h * 128:(h + 1) * 128]
            at = pl.ds(pl.multiple_of(i * 16 + h * 8, 8), 8)
            contrib[at, 0:128] = part[0:8]
            contrib[at, 128:256] = part[8:16]

    for copy in o_copies:
        copy.wait_recv()
    for v in range(nv):
        m = nv * lev // 2 // nv
        top = jnp.concatenate([o_dst[0], os_dst[0]], axis=1).astype(F32).reshape(pairs, 8, ocol + 128)
        bottom = jnp.concatenate([o_dst[1], os_dst[1]], axis=1).astype(F32).reshape(pairs, 8, ocol + 128)
        beside = om_dst[...].astype(F32).reshape(nv, lev, 8, 128)
        oext[v, :, 0:8, 0:ocol] = ocean_ref[v]
        oext[v, :, 0:8, ocol:] = beside[v]
        for q in range(m):
            first, second = halo_pair(top[v * m + q], bottom[v * m + q])
            oext[v, 2 * q, 8:16, :] = first
            oext[v, 2 * q + 1, 8:16, :] = second
        for t in range(2):
            oterms[v, :, :, t * 8:(t + 1) * 8, :] = mix(o_lhs[...], oext[v, :, t * 8:(t + 1) * 8, :])
    shape = (16, ocol + 128)
    r_at, c_at = lax.broadcasted_iota(I32, shape, 0), lax.broadcasted_iota(I32, shape, 1)
    no_up = (r_at == 0) & (j == 0)
    no_down = (r_at == 7) & (j == n_dom - 1)
    no_left = (c_at == 0) & (g == 0)
    no_right = (c_at == ocol - 1) & (g == n_grp - 1)
    at_once = nv * lev // parts
    per_v = lev // at_once

    def ocean_levels(c):
        v, base = c // per_v, lax.rem(c, per_v) * at_once
        state = [oext[v, base + q] for q in range(at_once)]
        for k in range(STEPS):
            for q in range(at_once):
                r = state[q]
                near = jnp.where(no_up, 0.0, pltpu.roll(r, 1, 0)) + jnp.where(no_down, 0.0, pltpu.roll(r, 15, 0))
                near = near + jnp.where(no_left, 0.0, pltpu.roll(r, 1, 1))
                near = near + jnp.where(no_right, 0.0, pltpu.roll(r, ocol + 127, 1))
                state[q] = diffuse * (r + near) + oterms[v, k, base + q]
        for q in range(at_once):
            oout_ref[v, base + q] = state[q][0:8, 0:ocol]

    def forward(c, carry):
        w_copy(c).wait()
        for s in range(per // 16):
            i = c * (per // 16) + s
            lhs = jnp.concatenate([spread_groups(tiles_f[2 * i]), spread_groups(tiles_f[2 * i + 1])], axis=0)
            both = w[pl.ds(i * 16, 16)].reshape(2, 1024, 128)
            keep(i, dot(lhs, jnp.concatenate([both[0], both[1]], axis=1)))
        ocean_levels(c)
        return carry

    lax.fori_loop(0, parts, forward, 0)

    chi, clo = split(contrib[...])
    for h in range(2):
        hot = (lax.broadcasted_iota(I32, (span, tiles), 0) + h * span == dest).astype(F32).astype(BF16)
        acc[h] = dot(hot, chi) + dot(hot, clo)
    p1 = remote(acc.at[1 - core], acc_in, p1_sem.at[0], p1_sem.at[1], partner)
    p1.start()
    strip_operator(a_lhs, alev_ref[...], rows)
    p1.wait_recv()
    own = acc[core] + acc_in[...]
    send2[...] = own.astype(BF16)

    def slot(ref, c):
        return ref.at[pl.ds(pl.multiple_of(c * obl, obl), obl)]

    def p2(k):
        c, who = peer(k)
        return remote(slot(send2, c), slot(inbox, chip), p2_send.at[c], p2_recv.at[chip], who)

    def p2_in(k):
        c, who = peer(k)
        return remote(slot(send2, c), slot(inbox, c), p2_send.at[c], p2_recv.at[c], who)

    def loop(f):
        def step(k, carry):
            f(k)
            return carry

        lax.fori_loop(1, nc, step, 0)

    loop(lambda k: p2(k).start())
    for copy in h_copies:
        copy.wait_recv()
    zeros = jnp.zeros((rows, 128), F32)
    width = 512

    def out_copy(v):
        return pltpu.make_async_copy(res.at[v], out_hbm.at[v], out_sem.at[v])

    def along_y(r):
        padded = jnp.concatenate([r, zeros], axis=1)
        return pltpu.roll(padded, 1, 1)[:, :cols] + pltpu.roll(padded, cols + 127, 1)[:, :cols]

    p4 = remote(flux_all.at[core], flux_all.at[core], p4_sem.at[0], p4_sem.at[1], partner)
    p4_in = remote(flux_all.at[1 - core], flux_all.at[1 - core], p4_sem.at[0], p4_sem.at[1], partner)

    def unpack(i, carry):
        at = pl.ds(pl.multiple_of(i * 16, 16), 16)
        high, low = halo_dst[0, at, :].astype(F32), halo_dst[1, at, :].astype(F32)
        for q in range(2):
            first, second = halo_pair(high[q * 8:(q + 1) * 8], low[q * 8:(q + 1) * 8])
            halo[4 * i + 2 * q] = first
            halo[4 * i + 2 * q + 1] = second
        return carry

    lax.fori_loop(0, nv * lev // 4, unpack, 0)
    pieces = cols // width
    group = lev // pieces

    def along_levels(v, c):
        at = pl.ds(pl.multiple_of(c * width, width), width)
        hi, lo = split(atm[v, :, :, at].reshape(lev * rows, width))
        beyond = halo[v * lev:(v + 1) * lev, :, at].reshape(lev * 8, width).astype(BF16)
        out = dot(a_lhs[...], jnp.concatenate([hi, lo, hi, beyond, beyond], axis=0))
        terms[v][:, :, :, at] = out.reshape(STEPS, lev, rows, width)

    def horner(v, c):
        for q in range(group):
            l = c * group + q
            r = diffuse ** STEPS * atm[v, l]
            for k in range(STEPS - 1, -1, -1):
                r = terms[v][k, l] + along_y(r)
            res[v, l] = r

    def stage(product, sums):
        def one(c, carry):
            if product is not None:
                along_levels(product, c)
            if sums is not None:
                horner(sums, c)
            return carry

        lax.fori_loop(0, pieces, one, 0)

    stage(0, None)
    mine = pl.ds(pl.multiple_of(chip * obl, obl), obl)
    loop(lambda k: p2_in(k).wait_recv())
    inbox[mine, :] = send2[mine, :]
    received = jnp.sum(inbox[...].astype(F32).reshape(nc, obl, nv * 128), axis=0)
    osurf = [
        jnp.concatenate([ocean_ref[v, 0, :, c * 128:(c + 1) * 128] for c in range(nch)], axis=0) for v in range(nv)
    ]
    flux = received - jnp.concatenate(osurf, axis=1)
    flux_all[core, mine, :] = flux.astype(BF16)

    def p3(k):
        c, who = peer(k)
        return remote(slot(flux_all.at[core], chip), slot(flux_all.at[core], chip), p3_send.at[c], p3_recv.at[chip], who)

    def p3_in(k):
        c, who = peer(k)
        return remote(slot(flux_all.at[core], c), slot(flux_all.at[core], c), p3_send.at[c], p3_recv.at[c], who)

    loop(lambda k: p3(k).start())

    for v in range(nv):
        field = jnp.concatenate([flux[c * 8:(c + 1) * 8, v * 128:(v + 1) * 128] for c in range(nch)], axis=1)
        oout_ref[v, 0] = oout_ref[v, 0] + couple * field

    for v in range(1, nv):
        stage(v, v - 1)
        out_copy(v - 1).start()
    loop(lambda k: p3_in(k).wait_recv())
    p4.start()
    stage(None, nv - 1)
    out_copy(nv - 1).start()
    p4_in.wait_recv()
    flux_ref[...] = flux_all[...].reshape(2 * span, nv * 128)
    for copy in o_copies + h_copies + [p1, p4]:
        copy.wait_send()
    loop(lambda k: p2(k).wait_send())
    loop(lambda k: p3(k).wait_send())
    for v in range(nv):
        out_copy(v).wait()


def back_body(
    obl, orow, nch,
    w_hbm, pre_hbm, opre_hbm, flux_ref, owner_ref, block_ref, source_ref, count_ref,
    out_hbm, oout_hbm,
    w, pre, opre, acc, contrib, ret,
    w_sem, in_sem, out_sem, o_sem,
):
    nv, lev, rows, cols = pre.shape
    tiles = w.shape[0]
    chunks = cols // 128
    span = flux_ref.shape[0] // 2
    half = w_sem.shape[0]
    per = tiles // half

    def w_copy(c):
        at = pl.ds(c * per, per)
        return pltpu.make_async_copy(w_hbm.at[at], w.at[at], w_sem.at[c])

    def first_in(v):
        return pltpu.make_async_copy(pre_hbm.at[v, 0], pre.at[v, 0], in_sem.at[v, 0])

    def rest_in(v):
        at = pl.ds(1, lev - 1)
        return pltpu.make_async_copy(pre_hbm.at[v, at], pre.at[v, at], in_sem.at[v, 1])

    def first_out(v):
        return pltpu.make_async_copy(pre.at[v, 0], out_hbm.at[v, 0], out_sem.at[v, 0])

    def rest_out(v):
        at = pl.ds(1, lev - 1)
        return pltpu.make_async_copy(pre.at[v, at], out_hbm.at[v, at], out_sem.at[v, 1])

    o_in = pltpu.make_async_copy(opre_hbm, opre, o_sem.at[0])
    o_out = pltpu.make_async_copy(opre, oout_hbm, o_sem.at[1])
    for c in range(half):
        w_copy(c).start()
    o_in.start()
    for v in range(nv):
        rest_in(v).start()
        first_in(v).start()

    _, place, dest_col, _ = tile_map(
        tiles, count_ref[0], owner_ref[...], block_ref[...], source_ref[...], span, obl, orow, nch, rows, chunks
    )
    hot = (lax.broadcasted_iota(I32, (tiles, 2 * span), 1) == dest_col).astype(F32).astype(BF16)
    values = dot(hot, flux_ref[...])
    column = within(lax.broadcasted_iota(I32, (128, 256), 1), 64)
    step, sub = 16, 4
    blank = jnp.zeros((128, 128), BF16)
    for q in range(tiles // 128):
        groups = []
        for h in range(2):
            at = q * 128 + h * 64
            both = jnp.concatenate([values[at:at + 64, v * 128:(v + 1) * 128] for v in range(nv)], axis=0)
            groups.append(both.T.astype(BF16))
        rhs = jnp.concatenate(
            [
                jnp.concatenate([groups[0], blank], axis=1),
                jnp.concatenate([blank, groups[1]], axis=1),
            ],
            axis=0,
        )
        for c in range(q * half * 128 // tiles, (q + 1) * half * 128 // tiles):
            w_copy(c).wait()
        acc[...] = jnp.zeros((128, 256), F32)

        def some(i, carry):
            total = acc[...]
            for s in range(0, step, sub):
                at = q * 128 + i * step + s
                first = w[pl.ds(at, sub)].reshape(sub * 128, 128)
                second = w[pl.ds(at + 64, sub)].reshape(sub * 128, 128)
                out = dot(jnp.concatenate([first, second], axis=1), rhs)
                for t in range(sub):
                    total = jnp.where(column == i * step + s + t, out[t * 128:(t + 1) * 128], total)
            acc[...] = total
            return carry

        lax.fori_loop(0, 64 // step, some, 0)
        turned = acc[...].T
        for h in range(2):
            for v in range(nv):
                at = h * 128 + v * 64
                contrib[q * 128 + h * 64:q * 128 + (h + 1) * 64, v * 128:(v + 1) * 128] = turned[at:at + 64]
        if q == 0:
            o_in.wait()
            o_out.start()
            for v in range(nv):
                rest_in(v).wait()
                rest_out(v).start()

    bhi, blo = split(contrib[...])
    to_block = (lax.broadcasted_iota(I32, (chunks * rows, tiles), 0) == place).astype(F32).astype(BF16)
    ret[...] = dot(to_block, bhi) + dot(to_block, blo)
    for v in range(nv):
        first_in(v).wait()
        field = jnp.concatenate(
            [ret[c * rows:(c + 1) * rows, v * 128:(v + 1) * 128] for c in range(chunks)], axis=1
        )
        pre[v, 0] = pre[v, 0] - couple * field
        first_out(v).start()
    o_out.wait()
    for v in range(nv):
        rest_out(v).wait()
        first_out(v).wait()


def solution(mesh):
    n_grp, n_dom = mesh.shape["grp"], mesh.shape["dom"]
    nc = n_grp * n_dom // 2

    def per_device(
        atm_state, ocean_state, atm_levels, ocean_levels, tile_weight, tile_owner, tile_block, tile_source, tile_count
    ):
        nv, lev, rows, cols = atm_state.shape
        tiles = tile_weight.shape[0]
        orow, ocol = ocean_state.shape[2:]
        obl = orow * ocol // 128
        pairs = nv * lev // 2
        lanes = nv * 128
        dma = pltpu.SemaphoreType.DMA
        vmem = pl.BlockSpec(memory_space=pltpu.VMEM)
        hbm = pl.BlockSpec(memory_space=pl.ANY)
        tile_args = (
            tile_owner.reshape(1, tiles), tile_block.reshape(1, tiles), tile_source.reshape(1, tiles), tile_count
        )
        smem = pl.BlockSpec(memory_space=pltpu.SMEM)
        span = nc * obl
        atm_pre, ocean_pre, flux = pl.pallas_call(
            functools.partial(body, (n_grp, n_dom)),
            out_shape=(
                jax.ShapeDtypeStruct(atm_state.shape, F32),
                jax.ShapeDtypeStruct(ocean_state.shape, F32),
                jax.ShapeDtypeStruct((2 * span, lanes), BF16),
            ),
            in_specs=[hbm, hbm, vmem, vmem, vmem, vmem, vmem, vmem, smem],
            out_specs=(hbm, vmem, vmem),
            scratch_shapes=[
                pltpu.VMEM(tile_weight.shape, BF16),
                pltpu.VMEM(atm_state.shape, F32),
                pltpu.VMEM(atm_state.shape, F32),
                pltpu.VMEM((2, pairs * 8, cols), BF16),
                pltpu.VMEM((2, pairs * 8, cols), BF16),
                pltpu.VMEM((nv * lev, 8, cols), F32),
                *[pltpu.VMEM((STEPS, lev, rows, cols), F32)] * nv,
                pltpu.VMEM((2, pairs * 8, ocol), BF16),
                pltpu.VMEM((2, pairs * 8, ocol), BF16),
                pltpu.VMEM((2, pairs * 8, 128), BF16),
                pltpu.VMEM((2, pairs * 8, 128), BF16),
                pltpu.VMEM((nv * lev * 8, 128), BF16),
                pltpu.VMEM((nv * lev * 8, 128), BF16),
                pltpu.VMEM((nv, lev, 16, ocol + 128), F32),
                pltpu.VMEM((nv, STEPS, lev, 16, ocol + 128), F32),
                pltpu.VMEM((STEPS * lev * 8, 3 * lev * 8), BF16),
                pltpu.VMEM((STEPS * lev * rows, 3 * lev * rows + 2 * lev * 8), BF16),
                pltpu.VMEM((tiles // 8, 8 * nv, 128), F32),
                pltpu.VMEM((tiles, lanes), F32),
                pltpu.VMEM((2, nc * obl, lanes), F32),
                pltpu.VMEM((nc * obl, lanes), F32),
                pltpu.VMEM((nc * obl, lanes), BF16),
                pltpu.VMEM((nc * obl, lanes), BF16),
                pltpu.VMEM((2, nc * obl, lanes), BF16),
                dma((4,)), dma((nv,)), dma((nv,)),
                dma((2,)), dma((2,)), dma((5,)), dma((5,)),
                dma((2,)), dma((nc,)), dma((nc,)), dma((nc,)), dma((nc,)), dma((2,)),
            ],
            compiler_params=pltpu.CompilerParams(
                collective_id=0, has_side_effects=True, vmem_limit_bytes=60 * 1024 * 1024
            ),
            cost_estimate=pl.CostEstimate(flops=8_000_000_000, bytes_accessed=17_000_000, transcendentals=0),
        )(
            tile_weight, atm_state, ocean_state, atm_levels, ocean_levels, *tile_args
        )
        return pl.pallas_call(
            functools.partial(back_body, obl, orow, ocol // 128),
            out_shape=(
                jax.ShapeDtypeStruct(atm_state.shape, F32),
                jax.ShapeDtypeStruct(ocean_state.shape, F32),
            ),
            in_specs=[hbm, hbm, hbm, vmem, vmem, vmem, vmem, smem],
            out_specs=(hbm, hbm),
            scratch_shapes=[
                pltpu.VMEM(tile_weight.shape, BF16),
                pltpu.VMEM(atm_state.shape, F32),
                pltpu.VMEM(ocean_state.shape, F32),
                pltpu.VMEM((128, 256), F32),
                pltpu.VMEM((tiles, lanes), F32),
                pltpu.VMEM((rows * cols // 128, lanes), F32),
                dma((4,)), dma((nv, 2)), dma((nv, 2)), dma((2,)),
            ],
            compiler_params=pltpu.CompilerParams(vmem_limit_bytes=60 * 1024 * 1024),
            cost_estimate=pl.CostEstimate(flops=2_000_000_000, bytes_accessed=17_000_000, transcendentals=0),
        )(tile_weight, atm_pre, ocean_pre, flux, *tile_args)

    in_specs = (
        P(None, None, ("grp", "dom"), None),
        P(None, None, "dom", "grp"),
        P(),
        P(),
        P(("grp", "dom"), None, None),
        P(("grp", "dom"), None),
        P(("grp", "dom")),
        P(("grp", "dom")),
        P(("grp", "dom")),
    )
    out_specs = (P(None, None, ("grp", "dom"), None), P(None, None, "dom", "grp"))
    return jax.shard_map(per_device, mesh=mesh, in_specs=in_specs, out_specs=out_specs, check_vma=False)
```
